512 devices in a mesh: inst: 32 (over x, z), head: 16 (over y, core).
Axes of the slice: x: 4, y: 8, z: 8, core: 2. Of those that a mesh axis runs over, the one named last changes fastest.
Arguments:
- hidden_rows: bfloat16 [32, 32, 16, 9216], P('inst', None, None, 'head'), may hold values from -6 to 6
- send_counts: int32 [32, 32], P('inst'), may hold values from 0 to 16, as said below
- row_session: int32 [32, 32, 16], P('inst'), may hold values from 0 to 1, as said below
- row_position: int32 [32, 32, 16], P('inst'), may hold values from 0 to 1023, as said below
- resident_lengths: int32 [64], P('inst'), may hold values from 1 to 512, as said below
- kv_weight: bfloat16 [9216, 12288], P('inst', 'head'), may hold values from -0.0625 to 0.0625
- key_cache: bfloat16 [64, 1024, 6144], P('inst', None, 'head'), as said below
- value_cache: bfloat16 [64, 1024, 6144], P('inst', None, 'head'), may hold values from -6 to 6
- query: bfloat16 [64, 6144], P('inst', 'head'), as said below
- new_key: bfloat16 [64, 6144], P('inst', 'head'), may hold values from -6 to 6
- new_value: bfloat16 [64, 6144], P('inst', 'head'), may hold values from -6 to 6
Outputs:
- attended: bfloat16 [64, 6144], P('inst', 'head')
The draws below stay inside these ranges and needn't reach their ends.
Inputs may be any that keep to these rules, and one draw needn't show every extreme that they name: `send_counts`: at most 16 live slots from one source to one destination; in every draw one destination instance receives 16 rows from every source. `row_session`: for a live slot, a session of the destination instance; 0 in slots that are not live. The destination that receives 16 rows from every source sends all of them to one of its sessions. `row_position`: the live rows of one destination session take each of the positions from its resident length to its resident length plus their number minus 1 exactly once; 0 in slots that are not live. In every draw some session's rows end at position 1023. `resident_lengths`: A session's resident length plus its restored rows stays within 1024 positions. `key_cache`: entries of order one. `query`: entries of order one or a few tens.
All inputs are finite; a program needn't handle non-finite values.
Results may differ from the reference program's by a relative error of at most 0.009.
Values may be sent and summed in bfloat16 or wider, within the bound.
No kernel may reach another device: no remote copies, remote signals or barrier semaphores. Data moves between devices by JAX's collectives and lax.ppermute only.
A program may use at most 192 MiB of HBM per device.

```python
import math
import jax
import jax.numpy as jnp
from jax import lax

D = 9216
HDIM = 128
SESS = 2
CTX = 1024
CAP = 16
INSTANCES = 32
HEADS = 48
SLOTS = 512


def restore_plan(key):
    drawn_key = jax.random.fold_in(key, 7)
    count_key, full_key, session_key, length_key, pick_key, step_key = jax.random.split(drawn_key, 6)
    counts = jax.random.randint(count_key, (INSTANCES, INSTANCES), 0, CAP + 1)
    busiest = jax.random.randint(full_key, (), 0, INSTANCES)
    counts = jnp.where(jnp.arange(INSTANCES)[None, :] == busiest, CAP, counts).astype(jnp.int32)
    busiest_session = jax.random.randint(pick_key, (), 0, SESS)
    session_total = INSTANCES * SESS
    lengths = jax.random.randint(length_key, (session_total,), 1, CTX - SLOTS + 1)
    longest_row = busiest * SESS + busiest_session
    shortest_row = (longest_row + 1 + jax.random.randint(step_key, (), 0, session_total - 1)) % session_total
    row_ids = jnp.arange(session_total)
    lengths = jnp.where(row_ids == longest_row, CTX - SLOTS, lengths)
    lengths = jnp.where(row_ids == shortest_row, 1, lengths).astype(jnp.int32)
    slot_live = jnp.arange(CAP)[None, None, :] < counts[:, :, None]
    sessions = jax.random.randint(session_key, (INSTANCES, INSTANCES, CAP), 0, SESS)
    sessions = jnp.where((jnp.arange(INSTANCES) == busiest)[None, :, None], busiest_session, sessions)
    live_dest = jnp.swapaxes(slot_live, 0, 1).reshape(INSTANCES, SLOTS)
    sess_dest = jnp.swapaxes(sessions, 0, 1).reshape(INSTANCES, SLOTS)
    member = ((sess_dest[:, :, None] == jnp.arange(SESS)[None, None, :]) & live_dest[:, :, None]).astype(jnp.int32)
    rank_before = jnp.cumsum(member, axis=1) - member
    rank_row = jnp.sum(rank_before * member, axis=2)
    first_pos = jnp.take_along_axis(lengths.reshape(INSTANCES, SESS), sess_dest, axis=1)
    positions = jnp.where(live_dest, first_pos + rank_row, 0)
    sess_out = jnp.where(live_dest, sess_dest, 0)
    positions = jnp.swapaxes(positions.reshape(INSTANCES, INSTANCES, CAP), 0, 1).astype(jnp.int32)
    sess_out = jnp.swapaxes(sess_out.reshape(INSTANCES, INSTANCES, CAP), 0, 1).astype(jnp.int32)
    return (counts, sess_out, positions, lengths)


def draw_send_counts(key, part):
    return restore_plan(key)[0]


def draw_row_session(key, part):
    return restore_plan(key)[1]


def draw_row_position(key, part):
    return restore_plan(key)[2]


def draw_resident_lengths(key, part):
    return restore_plan(key)[3]


def cache_keys(key):
    cache_shape = (INSTANCES * SESS, CTX, HEADS * HDIM)
    sub_key = jax.random.fold_in(key, 11)
    return jax.random.normal(sub_key, cache_shape, jnp.float32)


def draw_key_cache(key, part):
    return cache_keys(key).astype(jnp.bfloat16)


def draw_query(key, part):
    drawn = jax.random.normal(jax.random.fold_in(key, 13), (INSTANCES * SESS, HEADS * HDIM), jnp.float32)
    return drawn.astype(jnp.bfloat16)


def block_scale(stream_key, extent, cuts, low, largest):
    factor_of = 1.0
    for axis_at, shards_of in cuts:
        steps = jax.random.uniform(jax.random.fold_in(jax.random.fold_in(stream_key, 6), axis_at), (shards_of,), jnp.float32, low / len(cuts), largest / len(cuts))
        factor_of = factor_of * jnp.repeat(jnp.exp(steps), extent[axis_at] // shards_of).reshape((-1,) + (1,) * (len(extent) - 1 - axis_at))
    return factor_of


def centred(stream_key, dims, spread, bound, shards=(), held_as=jnp.bfloat16):
    result = spread * jax.random.normal(stream_key, dims, jnp.float32)
    if shards:
        result = result * block_scale(stream_key, dims, shards, -0.22, 0.18)
    return jnp.clip(result, -bound, bound).astype(held_as)


def setup_inputs(seed: int = 0) -> dict:
    key_of = jax.random.split(jax.random.key(seed), 12)
    hidden_rows = centred(key_of[0], (INSTANCES, INSTANCES, CAP, D), 1.0, 6.0, ((0, 32), (3, 16)))
    send_counts = draw_send_counts(jax.random.fold_in(key_of[11], 71), 0)
    row_session = draw_row_session(jax.random.fold_in(key_of[11], 71), 0)
    row_position = draw_row_position(jax.random.fold_in(key_of[11], 71), 0)
    resident_lengths = draw_resident_lengths(jax.random.fold_in(key_of[11], 71), 0)
    kv_weight = centred(key_of[5], (D, 2 * HEADS * HDIM), D ** -0.5, 0.0625, ((0, 32), (1, 16)))
    key_cache = draw_key_cache(jax.random.fold_in(key_of[11], 71), 0)
    value_cache = centred(key_of[7], (INSTANCES * SESS, CTX, HEADS * HDIM), 1.0, 6.0, ((0, 32), (2, 16)))
    query = draw_query(jax.random.fold_in(key_of[11], 71), 0)
    new_key = centred(key_of[9], (INSTANCES * SESS, HEADS * HDIM), 1.0, 6.0, ((0, 32), (1, 16)))
    new_value = centred(key_of[10], (INSTANCES * SESS, HEADS * HDIM), 1.0, 6.0, ((0, 32), (1, 16)))
    return {"hidden_rows": hidden_rows, "send_counts": send_counts, "row_session": row_session, "row_position": row_position, "resident_lengths": resident_lengths, "kv_weight": kv_weight, "key_cache": key_cache, "value_cache": value_cache, "query": query, "new_key": new_key, "new_value": new_value}


masked_score = -1e+30

def reference(hidden_rows, send_counts, row_session, row_position, resident_lengths, kv_weight, key_cache, value_cache, query, new_key, new_value):
    inverse_root = 1.0 / math.sqrt(HDIM)
    by_dest = jnp.swapaxes(hidden_rows, 0, 1).reshape(INSTANCES, SLOTS, D)
    slot_live = jnp.arange(CAP)[None, None, :] < send_counts[:, :, None]
    slot_live = jnp.swapaxes(slot_live, 0, 1).reshape(INSTANCES, SLOTS)
    session_map = jnp.swapaxes(row_session, 0, 1).reshape(INSTANCES, SLOTS).astype(jnp.int32)
    position_map = jnp.swapaxes(row_position, 0, 1).reshape(INSTANCES, SLOTS).astype(jnp.int32)
    cache_shape = (INSTANCES, SESS, CTX, HEADS, HDIM)
    group_shape = (INSTANCES, SESS, HEADS, HDIM)

    def per_instance(fields):
        hidden_now, live_now, sessions, positions, resident, key_rows, value_rows, queries, fresh_key, fresh_value = fields
        projected = jnp.dot(hidden_now, kv_weight, preferred_element_type=jnp.float32).astype(jnp.bfloat16)
        projected = projected.reshape(SLOTS, HEADS, 2, HDIM)
        target = jnp.where(live_now, positions, CTX).astype(jnp.int32)
        key_rows = key_rows.at[sessions, target].set(projected[:, :, 0], mode='drop')
        value_rows = value_rows.at[sessions, target].set(projected[:, :, 1], mode='drop')
        member = (sessions[None, :] == jnp.arange(SESS, dtype=jnp.int32)[:, None]) & live_now[None, :]
        totals = resident + lax.optimization_barrier(jnp.sum(member.astype(jnp.int32), axis=1))
        visible = jnp.arange(CTX, dtype=jnp.int32)[None, :] < totals[:, None]
        scores = jnp.einsum('shd,sphd->shp', queries.astype(jnp.float32), key_rows.astype(jnp.float32)) * inverse_root
        scores = jnp.where(visible[:, None, :], scores, masked_score)
        own_score = lax.optimization_barrier(jnp.sum(queries.astype(jnp.float32) * fresh_key.astype(jnp.float32), axis=-1)) * inverse_root
        highest = jnp.maximum(lax.optimization_barrier(jnp.max(scores, axis=-1)), own_score)
        weights = jnp.exp(scores - highest[:, :, None])
        own_weight = jnp.exp(own_score - highest)
        denominator = lax.optimization_barrier(jnp.sum(weights, axis=-1)) + own_weight
        probability = (weights / denominator[:, :, None]).astype(jnp.bfloat16)
        own_prob = (own_weight / denominator).astype(jnp.bfloat16)
        attended = jnp.einsum('shp,sphd->shd', probability.astype(jnp.float32), value_rows.astype(jnp.float32))
        attended = attended + own_prob.astype(jnp.float32)[:, :, None] * fresh_value.astype(jnp.float32)
        return attended.astype(jnp.bfloat16)
    results = lax.map(per_instance, (by_dest, slot_live, session_map, position_map, resident_lengths.reshape(INSTANCES, SESS), key_cache.reshape(cache_shape), value_cache.reshape(cache_shape), query.reshape(group_shape), new_key.reshape(group_shape), new_value.reshape(group_shape)))
    return results.reshape(INSTANCES * SESS, HEADS * HDIM)
```

```python
import math

import jax
import jax.numpy as jnp
from jax import lax
from jax.experimental import pallas as pl
from jax.experimental.pallas import tpu as pltpu
from jax.sharding import PartitionSpec as P

HDIM = 128
SESS = 2
RES_MAX = 512
ROWS = 8
LOW = -1e30
f32 = jnp.float32
bf16 = jnp.bfloat16
NT = (((1,), (1,)), ((), ()))


def iota(shape, dim):
    return lax.broadcasted_iota(jnp.int32, shape, dim)


def rows_of(shape, heads):
    row = iota(shape, len(shape) - 2) % ROWS
    u = (row >= heads).astype(jnp.int32)
    return u, row - u * heads


def vmem(n):
    return [pl.BlockSpec(memory_space=pltpu.VMEM)] * n


def pack_body(x_ref, q_ref, counts_ref, session_ref, out_ref):
    dests, cap, feats = x_ref.shape
    heads = q_ref.shape[1] // HDIM
    wide = heads * HDIM
    out_ref[:, :, 0:512] = x_ref[:, :, 0:512]
    q = q_ref[...].astype(f32)
    row = iota((cap, wide), 0)
    lane = iota((cap, wide), 1)
    spread = jnp.where(row < 8, q[0:1], q[1:2])
    spread = jnp.where((lane % HDIM) // 16 == row % 8, spread, 0.0)
    src = iota((wide, 64), 0)
    dst = iota((wide, 64), 1)
    fold = ((src // HDIM) * 16 + src % 16 == dst).astype(bf16)
    ext = jnp.dot(spread.astype(bf16), fold, preferred_element_type=f32)
    live = iota((cap, dests), 0) < counts_ref[...]
    code = jnp.where(live, 1 + session_ref[...], 0).astype(f32)
    at = iota((cap, 64), 1) == 48
    for i in range(dests):
        out_ref[i, :, feats : feats + 64] = jnp.where(at, code[:, i : i + 1], ext).astype(bf16)
    out_ref[:, :, 512:feats] = x_ref[:, :, 512:feats]


def qw_body(msg_ref, w_ref, out_ref, wk_ref):
    sources, cap, width = msg_ref.shape
    feats = w_ref.shape[0]
    heads = w_ref.shape[1] // (2 * HDIM)
    wide = heads * HDIM
    odd = lax.axis_index("inst") % 2
    wk_ref[...] = jnp.zeros_like(wk_ref)
    for parity in range(2):

        @pl.when(odd == parity)
        def _():
            for h in range(heads):
                wk_ref[parity * 32 : parity * 32 + feats, h * HDIM : (h + 1) * HDIM] = w_ref[
                    :, 2 * h * HDIM : (2 * h + 1) * HDIM
                ]

    n = sources * cap
    tail = msg_ref[:, :, width - 128 : width].reshape(n, 128)
    src = iota((128, wide), 0) - 64
    dst = iota((128, wide), 1)
    unfold = ((dst // HDIM) * 16 + dst % 16 == src).astype(bf16)
    z = jnp.dot(tail, unfold, preferred_element_type=f32)
    z = jnp.where((iota((n, wide), 1) % HDIM) // 16 == iota((n, wide), 0) % 8, z, 0.0).astype(bf16)
    m = sources * ROWS
    u, h = rows_of((m, n), heads)
    take = (iota((m, n), 0) // ROWS * 2 + u == iota((m, n), 1) // 8).astype(bf16)
    queries = jnp.dot(take, z, preferred_element_type=f32)
    u, h = rows_of((m, wide), heads)
    queries = jnp.where(iota((m, wide), 1) // HDIM == h, queries, 0.0).astype(bf16)
    out = lax.dot_general(queries, wk_ref[...], NT, preferred_element_type=f32)
    out_ref[...] = out.reshape(sources, ROWS, out.shape[1]).astype(bf16)


def cache_body(lengths_ref, q_ref, nk_ref, nv_ref, key_ref, value_ref, out_ref):
    heads = q_ref.shape[1] // HDIM
    wide = heads * HDIM
    span = key_ref.shape[1]
    root = 1.0 / math.sqrt(HDIM)
    u, h = rows_of((ROWS, wide), heads)
    mine = iota((ROWS, wide), 1) // HDIM == h
    q = q_ref[...].astype(f32)
    nk = nk_ref[...].astype(f32)
    nv = nv_ref[...].astype(f32)
    scores = jnp.zeros((ROWS, span), f32)
    own = jnp.zeros((ROWS, 1), f32)
    fresh = jnp.zeros((ROWS, wide), f32)
    for s in range(SESS):
        here = mine & (u == s)
        qs = jnp.where(here, q[s : s + 1], 0.0)
        scores += lax.dot_general(qs.astype(bf16), key_ref[s], NT, preferred_element_type=f32)
        own += jnp.sum(qs * nk[s : s + 1], axis=1, keepdims=True)
        fresh += jnp.where(here, nv[s : s + 1], 0.0)
    scores = scores * root
    us, _ = rows_of((ROWS, span), heads)
    length = jnp.where(us == 0, lengths_ref[0], lengths_ref[1])
    seen = iota((ROWS, span), 1) < length
    scores = jnp.where(seen, scores, LOW)
    top = jnp.max(scores, axis=1, keepdims=True)
    weight = jnp.where(seen, jnp.exp(scores - top), 0.0)
    total = jnp.sum(weight, axis=1, keepdims=True)
    high = weight.astype(bf16).astype(f32)
    both = jnp.concatenate([high, weight - high], axis=0)
    us2 = jnp.concatenate([us, us], axis=0)
    acc = jnp.zeros((2 * ROWS, wide), f32)
    for s in range(SESS):
        part = jnp.where(us2 == s, both, 0.0).astype(bf16)
        acc += jnp.dot(part, value_ref[s], preferred_element_type=f32)
    acc = jnp.where(mine, acc[:ROWS] + acc[ROWS:], 0.0)
    out = jnp.zeros((ROWS, HDIM), f32)
    new = jnp.zeros((ROWS, HDIM), f32)
    for k in range(heads):
        out += acc[:, k * HDIM : (k + 1) * HDIM]
        new += fresh[:, k * HDIM : (k + 1) * HDIM]
    out_ref[0] = out
    out_ref[1] = new
    lane = iota((ROWS, HDIM), 1)
    out_ref[2] = jnp.where(lane == 0, top, jnp.where(lane == 1, total, own * root))


def score_body(qx_ref, msg_ref, out_ref, code_ref):
    sources, cap, width = msg_ref.shape
    n = sources * cap
    blocks = qx_ref.shape[0] // 2
    heads = (ROWS - 2) // SESS
    pad = qx_ref.shape[2]
    q = qx_ref[...].astype(f32).reshape(blocks, 2, ROWS, pad)
    s = jnp.zeros((blocks * ROWS, n), f32)
    for half, at in ((0, 0), (1, width - pad)):
        a = q[:, half].reshape(blocks * ROWS, pad).astype(bf16)
        b = msg_ref[:, :, at : at + pad].reshape(n, pad)
        s += lax.dot_general(a, b, NT, preferred_element_type=f32)
    tail = msg_ref[:, :, width - 128 : width].reshape(n, 128)
    one = (iota((ROWS, 128), 1) == 64 + 48).astype(bf16)
    code = lax.dot_general(one, tail, NT, preferred_element_type=f32)
    code_ref[...] = code
    s = s.reshape(blocks, ROWS, n)
    out_ref[:, 0:heads, :] = jnp.where(code[None, 0:heads] == 2.0, s[:, heads : 2 * heads], s[:, 0:heads])
    out_ref[:, heads : heads + 1, :] = jnp.zeros((blocks, 1, n), f32)


def soft_body(parts_ref, code_ref, cache_ref, out_ref, base_ref):
    heads = (ROWS - 2) // SESS
    n = code_ref.shape[1]
    root = 1.0 / math.sqrt(HDIM)
    s = jnp.sum(parts_ref[...], axis=0) * root
    s = jnp.concatenate([s[0:heads], s[0:heads], s[0:2]], axis=0)
    u, h = rows_of((ROWS, n), heads)
    seen = code_ref[...] == (1 + u).astype(f32)
    s = jnp.where(seen, s, LOW)
    stats = cache_ref[2]
    top_c, total_c, own = stats[:, 0:1], stats[:, 1:2], stats[:, 2:3]
    top = jnp.maximum(jnp.maximum(top_c, own), jnp.max(s, axis=1, keepdims=True))
    weight = jnp.where(seen, jnp.exp(s - top), 0.0)
    scale_c = jnp.exp(top_c - top)
    own_w = jnp.exp(own - top)
    den = jnp.sum(weight, axis=1, keepdims=True) + total_c * scale_c + own_w
    prob = jnp.where(iota((ROWS, n), 0) < SESS * heads, weight / den, 0.0)
    out_ref[...] = jnp.broadcast_to(prob[None], out_ref.shape).astype(bf16)
    own_p = (own_w / den).astype(bf16).astype(f32)
    base_ref[...] = cache_ref[0] * (scale_c / den) + own_p * cache_ref[1]


def mix_body(prob_ref, msg_ref, out_ref):
    sources, cap, width = msg_ref.shape
    n = sources * cap
    blocks = prob_ref.shape[0]
    pad = out_ref.shape[3]
    p = prob_ref[...].astype(f32).reshape(blocks * ROWS, n).astype(bf16)
    for half, at in ((0, 0), (1, width - pad)):
        y = jnp.dot(p, msg_ref[:, :, at : at + pad].reshape(n, pad), preferred_element_type=f32)
        out_ref[:, half] = y.reshape(blocks, ROWS, pad).astype(bf16)


def value_body(y_ref, w_ref, out_ref, wv_ref):
    dests, _, pad = y_ref.shape
    feats = w_ref.shape[0]
    heads = w_ref.shape[1] // (2 * HDIM)
    odd = lax.axis_index("inst") % 2
    wv_ref[...] = jnp.zeros_like(wv_ref)
    for parity in range(2):

        @pl.when(odd == parity)
        def _():
            for h in range(heads):
                wv_ref[parity * 32 : parity * 32 + feats, h * HDIM : (h + 1) * HDIM] = w_ref[
                    :, (2 * h + 1) * HDIM : (2 * h + 2) * HDIM
                ]

    m = dests * ROWS
    y = y_ref[...].astype(f32).reshape(m, pad).astype(bf16)
    r = jnp.dot(y, wv_ref[...], preferred_element_type=f32)
    _, h = rows_of((m, HDIM), heads)
    out = jnp.zeros((m, HDIM), f32)
    for k in range(heads):
        out = jnp.where(h == k, r[:, k * HDIM : (k + 1) * HDIM], out)
    out_ref[...] = out.reshape(dests, ROWS, HDIM)


def last_body(parts_ref, base_ref, out_ref):
    heads = out_ref.shape[1] // HDIM
    t = jnp.sum(parts_ref[...], axis=0) + base_ref[...]
    for h in range(heads):
        both = jnp.concatenate([t[h : h + 1], t[heads + h : heads + h + 1]], axis=0)
        out_ref[:, h * HDIM : (h + 1) * HDIM] = both.astype(bf16)


def local(
    hidden_rows,
    send_counts,
    row_session,
    row_position,
    resident_lengths,
    kv_weight,
    key_cache,
    value_cache,
    query,
    new_key,
    new_value,
):
    _, insts, cap, feats = hidden_rows.shape
    wide = query.shape[1]
    slots = insts * cap
    blocks = lax.axis_size("head")
    pad = 3 * HDIM
    width = feats + 64
    swap = lambda t, axis: lax.all_to_all(t, axis, split_axis=0, concat_axis=0, tiled=True)

    msg = pl.pallas_call(
        pack_body,
        out_shape=jax.ShapeDtypeStruct((insts, cap, width), bf16),
        in_specs=vmem(4),
        out_specs=vmem(1)[0],
    )(hidden_rows[0], query, send_counts, row_session[0].T)
    msg = swap(msg, "inst")

    cache = pl.pallas_call(
        cache_body,
        grid=(1,),
        out_shape=jax.ShapeDtypeStruct((3, ROWS, HDIM), f32),
        in_specs=[pl.BlockSpec(memory_space=pltpu.SMEM)]
        + vmem(3)
        + [pl.BlockSpec((SESS, RES_MAX, wide), lambda i: (0, 0, 0))] * 2,
        out_specs=vmem(1)[0],
    )(resident_lengths, query, new_key, new_value, key_cache, value_cache)

    qw = pl.pallas_call(
        qw_body,
        out_shape=jax.ShapeDtypeStruct((insts, ROWS, pad), bf16),
        in_specs=vmem(2),
        out_specs=vmem(1)[0],
        scratch_shapes=[pltpu.VMEM((pad, wide), bf16)],
    )(msg, kv_weight)
    qx = swap(swap(qw, "inst"), "head")

    part, code = pl.pallas_call(
        score_body,
        out_shape=(
            jax.ShapeDtypeStruct((blocks, 4, slots), f32),
            jax.ShapeDtypeStruct((ROWS, slots), f32),
        ),
        in_specs=vmem(2),
        out_specs=tuple(vmem(2)),
    )(qx, msg)
    part = swap(part, "head")

    prob, base = pl.pallas_call(
        soft_body,
        out_shape=(
            jax.ShapeDtypeStruct((blocks, ROWS, slots), bf16),
            jax.ShapeDtypeStruct((ROWS, HDIM), f32),
        ),
        in_specs=vmem(3),
        out_specs=tuple(vmem(2)),
    )(part, code, cache)
    prob = swap(prob, "head")

    y = pl.pallas_call(
        mix_body,
        out_shape=jax.ShapeDtypeStruct((blocks, 2, ROWS, pad), bf16),
        in_specs=vmem(2),
        out_specs=vmem(1)[0],
    )(prob, msg)
    y = swap(swap(y.reshape(insts, ROWS, pad), "head"), "inst")

    out = pl.pallas_call(
        value_body,
        out_shape=jax.ShapeDtypeStruct((insts, ROWS, HDIM), f32),
        in_specs=vmem(2),
        out_specs=vmem(1)[0],
        scratch_shapes=[pltpu.VMEM((pad, wide), bf16)],
    )(y, kv_weight)
    out = swap(out, "inst")

    return pl.pallas_call(
        last_body,
        out_shape=jax.ShapeDtypeStruct((SESS, wide), bf16),
        in_specs=vmem(2),
        out_specs=vmem(1)[0],
    )(out, base)


def solution(mesh):
    placed = (
        P("inst", None, None, "head"),
        P("inst", None),
        P("inst", None, None),
        P("inst", None, None),
        P("inst"),
        P("inst", "head"),
        P("inst", None, "head"),
        P("inst", None, "head"),
        P("inst", "head"),
        P("inst", "head"),
        P("inst", "head"),
    )
    return jax.shard_map(
        local, mesh=mesh, in_specs=placed, out_specs=P("inst", "head"), check_vma=False
    )
```

```python
import math

import jax
import jax.numpy as jnp
from jax import lax
from jax.experimental import pallas as pl
from jax.experimental.pallas import tpu as pltpu
from jax.sharding import PartitionSpec as P

HDIM = 128
SESS = 2
RES_MAX = 512
ROWS = 8
LOW = -1e30
f32 = jnp.float32
bf16 = jnp.bfloat16
NT = (((1,), (1,)), ((), ()))


def iota(shape, dim):
    return lax.broadcasted_iota(jnp.int32, shape, dim)


def rows_of(shape, heads):
    row = iota(shape, len(shape) - 2) % ROWS
    u = (row >= heads).astype(jnp.int32)
    return u, row - u * heads


def vmem(n):
    return [pl.BlockSpec(memory_space=pltpu.VMEM)] * n


def pack_body(x_ref, q_ref, counts_ref, session_ref, out_ref):
    dests, cap, feats = x_ref.shape
    heads = q_ref.shape[1] // HDIM
    wide = heads * HDIM
    out_ref[:, :, 0:256] = x_ref[:, :, 0:256]
    out_ref[:, :, 256:512] = x_ref[:, :, 288:544]
    q = q_ref[...].astype(f32)
    row = iota((cap, wide), 0)
    lane = iota((cap, wide), 1)
    spread = jnp.where(row < 8, q[0:1], q[1:2])
    spread = jnp.where((lane % HDIM) // 16 == row % 8, spread, 0.0)
    src = iota((wide, 128), 0)
    dst = iota((wide, 128), 1) - 64
    fold = ((src // HDIM) * 16 + src % 16 == dst).astype(bf16)
    ext = jnp.dot(spread.astype(bf16), fold, preferred_element_type=f32)
    live = iota((cap, dests), 0) < counts_ref[...]
    code = jnp.where(live, 1 + session_ref[...], 0).astype(f32)
    lane = iota((cap, 128), 1)
    none = jnp.zeros((cap, 128 - (feats - 512)), f32)
    for i in range(dests):
        low = x_ref[i, :, 256:384].astype(f32)
        high = jnp.concatenate([x_ref[i, :, 512:feats].astype(f32), none], axis=1)
        t = jnp.where(lane == 64 + 48, code[:, i : i + 1], ext)
        t = jnp.where(lane < 32, low, jnp.where(lane < 64, high, t))
        out_ref[i, :, 512:640] = t.astype(bf16)


def qw_body(msg_ref, w_ref, out_ref, wk_ref):
    sources, cap, _ = msg_ref.shape
    heads = w_ref.shape[1] // (2 * HDIM)
    wide = heads * HDIM
    odd = lax.axis_index("inst") % 2
    wk_ref[...] = jnp.zeros_like(wk_ref)
    for parity in range(2):

        @pl.when(odd == parity)
        def _():
            for h in range(heads):
                at = 256 + parity * 32
                mine = slice(h * HDIM, (h + 1) * HDIM)
                keys = slice(2 * h * HDIM, (2 * h + 1) * HDIM)
                wk_ref[0:256, mine] = w_ref[0:256, keys]
                wk_ref[at : at + 32, mine] = w_ref[256:288, keys]

    n = sources * cap
    tail = msg_ref[...].reshape(n, 128)
    src = iota((128, wide), 0) - 64
    dst = iota((128, wide), 1)
    unfold = ((dst // HDIM) * 16 + dst % 16 == src).astype(bf16)
    z = jnp.dot(tail, unfold, preferred_element_type=f32)
    z = jnp.where((iota((n, wide), 1) % HDIM) // 16 == iota((n, wide), 0) % 8, z, 0.0).astype(bf16)
    m = sources * ROWS
    u, h = rows_of((m, n), heads)
    take = (iota((m, n), 0) // ROWS * 2 + u == iota((m, n), 1) // 8).astype(bf16)
    queries = jnp.dot(take, z, preferred_element_type=f32)
    u, h = rows_of((m, wide), heads)
    queries = jnp.where(iota((m, wide), 1) // HDIM == h, queries, 0.0).astype(bf16)
    out = lax.dot_general(queries, wk_ref[...], NT, preferred_element_type=f32)
    out_ref[...] = out.reshape(sources, ROWS, out.shape[1]).astype(bf16)


def cache_body(lengths_ref, q_ref, nk_ref, nv_ref, key_ref, value_ref, out_ref):
    heads = q_ref.shape[1] // HDIM
    wide = heads * HDIM
    span = key_ref.shape[1]
    root = 1.0 / math.sqrt(HDIM)
    u, h = rows_of((ROWS, wide), heads)
    mine = iota((ROWS, wide), 1) // HDIM == h
    q = q_ref[...].astype(f32)
    nk = nk_ref[...].astype(f32)
    nv = nv_ref[...].astype(f32)
    scores = jnp.zeros((ROWS, span), f32)
    own = jnp.zeros((ROWS, 1), f32)
    fresh = jnp.zeros((ROWS, wide), f32)
    for s in range(SESS):
        here = mine & (u == s)
        qs = jnp.where(here, q[s : s + 1], 0.0)
        scores += lax.dot_general(qs.astype(bf16), key_ref[s], NT, preferred_element_type=f32)
        own += jnp.sum(qs * nk[s : s + 1], axis=1, keepdims=True)
        fresh += jnp.where(here, nv[s : s + 1], 0.0)
    scores = scores * root
    us, _ = rows_of((ROWS, span), heads)
    length = jnp.where(us == 0, lengths_ref[0], lengths_ref[1])
    seen = iota((ROWS, span), 1) < length
    scores = jnp.where(seen, scores, LOW)
    top = jnp.max(scores, axis=1, keepdims=True)
    weight = jnp.where(seen, jnp.exp(scores - top), 0.0)
    total = jnp.sum(weight, axis=1, keepdims=True)
    high = weight.astype(bf16).astype(f32)
    both = jnp.concatenate([high, weight - high], axis=0)
    us2 = jnp.concatenate([us, us], axis=0)
    acc = jnp.zeros((2 * ROWS, wide), f32)
    for s in range(SESS):
        part = jnp.where(us2 == s, both, 0.0).astype(bf16)
        acc += jnp.dot(part, value_ref[s], preferred_element_type=f32)
    acc = jnp.where(mine, acc[:ROWS] + acc[ROWS:], 0.0)
    out = jnp.zeros((ROWS, HDIM), f32)
    new = jnp.zeros((ROWS, HDIM), f32)
    for k in range(heads):
        out += acc[:, k * HDIM : (k + 1) * HDIM]
        new += fresh[:, k * HDIM : (k + 1) * HDIM]
    out_ref[0] = out
    out_ref[1] = new
    lane = iota((ROWS, HDIM), 1)
    out_ref[2] = jnp.where(lane == 0, top, jnp.where(lane == 1, total, own * root))


def score_body(qx_ref, msg_ref, out_ref, code_ref):
    sources, cap, width = msg_ref.shape
    n = sources * cap
    blocks = qx_ref.shape[0] // 2
    heads = (ROWS - 2) // SESS
    pad = qx_ref.shape[2]
    q = qx_ref[...].astype(f32).reshape(blocks, 2, ROWS, pad)
    a = jnp.concatenate([q[:, 0, :, 0:256], q[:, 1, :, 0:256], q[:, 0, :, 256:pad] + q[:, 1, :, 256:pad]], axis=-1)
    a = a.reshape(blocks * ROWS, width).astype(bf16)
    s = lax.dot_general(a, msg_ref[...].reshape(n, width), NT, preferred_element_type=f32)
    tail = msg_ref[:, :, width - 128 : width].reshape(n, 128)
    one = (iota((ROWS, 128), 1) == 64 + 48).astype(bf16)
    code = lax.dot_general(one, tail, NT, preferred_element_type=f32)
    code_ref[...] = code
    s = s.reshape(blocks, ROWS, n)
    out_ref[:, 0:heads, :] = jnp.where(code[None, 0:heads] == 2.0, s[:, heads : 2 * heads], s[:, 0:heads])
    out_ref[:, heads : heads + 1, :] = jnp.zeros((blocks, 1, n), f32)


def soft_body(parts_ref, code_ref, cache_ref, out_ref, base_ref):
    heads = (ROWS - 2) // SESS
    n = code_ref.shape[1]
    root = 1.0 / math.sqrt(HDIM)
    s = jnp.sum(parts_ref[...], axis=0) * root
    s = jnp.concatenate([s[0:heads], s[0:heads], s[0:2]], axis=0)
    u, h = rows_of((ROWS, n), heads)
    seen = code_ref[...] == (1 + u).astype(f32)
    s = jnp.where(seen, s, LOW)
    stats = cache_ref[2]
    top_c, total_c, own = stats[:, 0:1], stats[:, 1:2], stats[:, 2:3]
    top = jnp.maximum(jnp.maximum(top_c, own), jnp.max(s, axis=1, keepdims=True))
    weight = jnp.where(seen, jnp.exp(s - top), 0.0)
    scale_c = jnp.exp(top_c - top)
    own_w = jnp.exp(own - top)
    den = jnp.sum(weight, axis=1, keepdims=True) + total_c * scale_c + own_w
    prob = jnp.where(iota((ROWS, n), 0) < SESS * heads, weight / den, 0.0)
    out_ref[...] = jnp.broadcast_to(prob[None], out_ref.shape).astype(bf16)
    own_p = (own_w / den).astype(bf16).astype(f32)
    base_ref[...] = cache_ref[0] * (scale_c / den) + own_p * cache_ref[1]


def mix_body(prob_ref, msg_ref, out_ref):
    sources, cap, width = msg_ref.shape
    n = sources * cap
    blocks = prob_ref.shape[0]
    p = prob_ref[...].astype(f32).reshape(blocks * ROWS, n).astype(bf16)
    y = jnp.dot(p, msg_ref[...].reshape(n, width), preferred_element_type=f32)
    out_ref[...] = y.reshape(blocks, ROWS, width).astype(bf16)


def last_body(y_ref, w_ref, base_ref, out_ref, most_ref, rest_ref, most_sem, rest_sem):
    blocks, _, width = y_ref.shape
    heads = out_ref.shape[1] // HDIM
    feats = w_ref.shape[0] // (2 * blocks)
    copies = []
    for a in range(2 * blocks):
        most = pltpu.make_async_copy(
            w_ref.at[pl.ds(a * feats, 256)], most_ref.at[pl.ds(a * 256, 256)], most_sem.at[a]
        )
        rest = pltpu.make_async_copy(
            w_ref.at[pl.ds(a * feats + 256, 32)],
            rest_ref.at[pl.ds((a // 2) * 128 + (a % 2) * 32, 32)],
            rest_sem.at[a],
        )
        most.start()
        rest.start()
        copies.append((most, rest))
    for j in range(blocks):
        rest_ref[j * 128 + 64 : j * 128 + 128] = jnp.zeros((64, rest_ref.shape[1]), bf16)
    r = jnp.zeros((ROWS, rest_ref.shape[1]), f32)
    for j in range(blocks):
        for a in (2 * j, 2 * j + 1):
            copies[a][0].wait()
            copies[a][1].wait()
        y = y_ref[j].astype(f32).astype(bf16)
        r += jnp.dot(y[:, 0:512], most_ref[j * 512 : (j + 1) * 512], preferred_element_type=f32)
        r += jnp.dot(y[:, 512:width], rest_ref[j * 128 : (j + 1) * 128], preferred_element_type=f32)
    _, h = rows_of((ROWS, HDIM), heads)
    t = base_ref[...]
    for k in range(heads):
        t += jnp.where(h == k, r[:, k * HDIM : (k + 1) * HDIM], 0.0)
    for k in range(heads):
        both = jnp.concatenate([t[k : k + 1], t[heads + k : heads + k + 1]], axis=0)
        out_ref[:, k * HDIM : (k + 1) * HDIM] = both.astype(bf16)


def local(
    hidden_rows,
    send_counts,
    row_session,
    row_position,
    resident_lengths,
    kv_weight,
    key_cache,
    value_cache,
    query,
    new_key,
    new_value,
):
    _, insts, cap, feats = hidden_rows.shape
    wide = query.shape[1]
    slots = insts * cap
    blocks = lax.axis_size("head")
    pad = 3 * HDIM
    width = feats + 64
    swap = lambda t, axis: lax.all_to_all(t, axis, split_axis=0, concat_axis=0, tiled=True)

    values = jnp.concatenate([kv_weight[:, k + HDIM : k + 2 * HDIM] for k in range(0, 2 * wide, 2 * HDIM)], axis=1)
    values = lax.all_gather(values, "inst", axis=0, tiled=True)

    msg = pl.pallas_call(
        pack_body,
        out_shape=jax.ShapeDtypeStruct((insts, cap, width), bf16),
        in_specs=vmem(4),
        out_specs=vmem(1)[0],
    )(hidden_rows[0], query, send_counts, row_session[0].T)
    msg = swap(msg, "inst")

    cache = pl.pallas_call(
        cache_body,
        grid=(1,),
        out_shape=jax.ShapeDtypeStruct((3, ROWS, HDIM), f32),
        in_specs=[pl.BlockSpec(memory_space=pltpu.SMEM)]
        + vmem(3)
        + [pl.BlockSpec((SESS, RES_MAX, wide), lambda i: (0, 0, 0))] * 2,
        out_specs=vmem(1)[0],
    )(resident_lengths, query, new_key, new_value, key_cache, value_cache)

    qw = pl.pallas_call(
        qw_body,
        grid=(1,),
        out_shape=jax.ShapeDtypeStruct((insts, ROWS, pad), bf16),
        in_specs=[pl.BlockSpec((insts, cap, 128), lambda i: (0, 0, width // 128 - 1)), vmem(1)[0]],
        out_specs=vmem(1)[0],
        scratch_shapes=[pltpu.VMEM((pad, wide), bf16)],
    )(msg, kv_weight)
    qx = swap(swap(qw, "inst"), "head")

    part, code = pl.pallas_call(
        score_body,
        out_shape=(
            jax.ShapeDtypeStruct((blocks, 4, slots), f32),
            jax.ShapeDtypeStruct((ROWS, slots), f32),
        ),
        in_specs=vmem(2),
        out_specs=tuple(vmem(2)),
    )(qx, msg)
    part = swap(part, "head")

    prob, base = pl.pallas_call(
        soft_body,
        out_shape=(
            jax.ShapeDtypeStruct((blocks, ROWS, slots), bf16),
            jax.ShapeDtypeStruct((ROWS, HDIM), f32),
        ),
        in_specs=vmem(3),
        out_specs=tuple(vmem(2)),
    )(part, code, cache)
    prob = swap(prob, "head")

    y = pl.pallas_call(
        mix_body,
        out_shape=jax.ShapeDtypeStruct((blocks, ROWS, width), bf16),
        in_specs=vmem(2),
        out_specs=vmem(1)[0],
    )(prob, msg)
    y = swap(y, "head")

    return pl.pallas_call(
        last_body,
        out_shape=jax.ShapeDtypeStruct((SESS, wide), bf16),
        in_specs=[vmem(1)[0], pl.BlockSpec(memory_space=pl.ANY), vmem(1)[0]],
        out_specs=vmem(1)[0],
        scratch_shapes=[
            pltpu.VMEM((insts * 256, wide), bf16),
            pltpu.VMEM((blocks * 128, wide), bf16),
            pltpu.SemaphoreType.DMA((insts,)),
            pltpu.SemaphoreType.DMA((insts,)),
        ],
        compiler_params=pltpu.CompilerParams(vmem_limit_bytes=56 * 2**20),
    )(y, values, base)


def solution(mesh):
    placed = (
        P("inst", None, None, "head"),
        P("inst", None),
        P("inst", None, None),
        P("inst", None, None),
        P("inst"),
        P("inst", "head"),
        P("inst", None, "head"),
        P("inst", None, "head"),
        P("inst", "head"),
        P("inst", "head"),
        P("inst", "head"),
    )
    return jax.shard_map(
        local, mesh=mesh, in_specs=placed, out_specs=P("inst", "head"), check_vma=False
    )
```

```python
import math

import jax
import jax.numpy as jnp
from jax import lax
from jax.experimental import pallas as pl
from jax.experimental.pallas import tpu as pltpu
from jax.sharding import PartitionSpec as P

HDIM = 128
SESS = 2
RES_MAX = 512
ROWS = 8
GROUP = 4
LOW = -1e30
f32 = jnp.float32
bf16 = jnp.bfloat16
NT = (((1,), (1,)), ((), ()))


def iota(shape, dim):
    return lax.broadcasted_iota(jnp.int32, shape, dim)


def rows_of(shape):
    row = iota(shape, len(shape) - 2) % ROWS
    return row // GROUP, row % GROUP


def spare_row(t, heads, part):
    u, h = rows_of(t.shape)
    own = jnp.where(u == 0, t[..., heads : heads + 1, :], t[..., GROUP + heads : GROUP + heads + 1, :])
    return jnp.where(iota(t.shape, t.ndim - 1) // part == h, own, 0.0)


def vmem(n):
    return [pl.BlockSpec(memory_space=pltpu.VMEM)] * n


def pack_body(x_ref, q_ref, counts_ref, session_ref, out_ref):
    dests, cap, feats = x_ref.shape
    heads = q_ref.shape[1] // HDIM
    wide = heads * HDIM
    out_ref[:, :, 0:256] = x_ref[:, :, 0:256]
    out_ref[:, :, 256:512] = x_ref[:, :, 288:544]
    q = q_ref[...].astype(f32)
    row = iota((cap, wide), 0)
    lane = iota((cap, wide), 1)
    spread = jnp.where(row < 8, q[0:1], q[1:2])
    spread = jnp.where((lane % HDIM) // 16 == row % 8, spread, 0.0)
    src = iota((wide, 128), 0)
    dst = iota((wide, 128), 1) - 64
    fold = ((src // HDIM) * 16 + src % 16 == dst).astype(bf16)
    ext = jnp.dot(spread.astype(bf16), fold, preferred_element_type=f32)
    live = iota((cap, dests), 0) < counts_ref[...]
    code = jnp.where(live, 1 + session_ref[...], 0).astype(f32)
    lane = iota((cap, 128), 1)
    none = jnp.zeros((cap, 128 - (feats - 512)), f32)
    for i in range(dests):
        low = x_ref[i, :, 256:384].astype(f32)
        high = jnp.concatenate([x_ref[i, :, 512:feats].astype(f32), none], axis=1)
        t = jnp.where(lane == 64 + 48, code[:, i : i + 1], ext)
        t = jnp.where(lane < 32, low, jnp.where(lane < 64, high, t))
        out_ref[i, :, 512:640] = t.astype(bf16)


def qw_body(msg_ref, w_ref, out_ref, odd_ref):
    sources, cap, _ = msg_ref.shape
    heads = w_ref.shape[1] // (2 * HDIM)
    wide = heads * HDIM
    odd_ref[...] = jnp.zeros_like(odd_ref)
    for h in range(heads):
        odd_ref[h * 32 : h * 32 + 32, h * HDIM : (h + 1) * HDIM] = w_ref[256:288, 2 * h * HDIM : (2 * h + 1) * HDIM]
    keys = jnp.concatenate([w_ref[0:256, 2 * h * HDIM : (2 * h + 1) * HDIM] for h in range(heads)], axis=1)

    n = sources * cap
    tail = msg_ref[...].reshape(n, 128)
    src = iota((128, wide), 0) - 64
    dst = iota((128, wide), 1)
    unfold = ((dst // HDIM) * 16 + dst % 16 == src).astype(bf16)
    z = jnp.dot(tail, unfold, preferred_element_type=f32)
    z = jnp.where((iota((n, wide), 1) % HDIM) // 16 == iota((n, wide), 0) % 8, z, 0.0).astype(bf16)
    m = sources * ROWS
    take = (iota((m, n), 0) // GROUP == iota((m, n), 1) // 8).astype(bf16)
    queries = jnp.dot(take, z, preferred_element_type=f32)
    _, h = rows_of((m, wide))
    queries = jnp.where((iota((m, wide), 1) // HDIM == h) | (h == heads), queries, 0.0).astype(bf16)
    even = lax.dot_general(queries, keys, NT, preferred_element_type=f32)
    odd = lax.dot_general(queries, odd_ref[...], NT, preferred_element_type=f32)
    _, h = rows_of((m, 128))
    first = jnp.where(h == heads, odd, even[:, 0:128])
    out_ref[:, :, 0:128] = first.reshape(sources, ROWS, 128).astype(bf16)
    out_ref[:, :, 128:256] = even[:, 128:256].reshape(sources, ROWS, 128).astype(bf16)


def cache_body(lengths_ref, q_ref, nk_ref, nv_ref, key_ref, value_ref, out_ref):
    heads = q_ref.shape[1] // HDIM
    wide = heads * HDIM
    span = key_ref.shape[1]
    root = 1.0 / math.sqrt(HDIM)
    u, h = rows_of((ROWS, wide))
    mine = iota((ROWS, wide), 1) // HDIM == h
    q = q_ref[...].astype(f32)
    nk = nk_ref[...].astype(f32)
    nv = nv_ref[...].astype(f32)
    scores = jnp.zeros((ROWS, span), f32)
    own = jnp.zeros((ROWS, 1), f32)
    fresh = jnp.zeros((ROWS, wide), f32)
    for s in range(SESS):
        here = mine & (u == s)
        qs = jnp.where(here, q[s : s + 1], 0.0)
        scores += lax.dot_general(qs.astype(bf16), key_ref[s], NT, preferred_element_type=f32)
        own += jnp.sum(qs * nk[s : s + 1], axis=1, keepdims=True)
        fresh += jnp.where(here, nv[s : s + 1], 0.0)
    scores = scores * root
    us, _ = rows_of((ROWS, span))
    length = jnp.where(us == 0, lengths_ref[0], lengths_ref[1])
    seen = iota((ROWS, span), 1) < length
    scores = jnp.where(seen, scores, LOW)
    top = jnp.max(scores, axis=1, keepdims=True)
    weight = jnp.where(seen, jnp.exp(scores - top), 0.0)
    total = jnp.sum(weight, axis=1, keepdims=True)
    high = weight.astype(bf16).astype(f32)
    both = jnp.concatenate([high, weight - high], axis=0)
    us2 = jnp.concatenate([us, us], axis=0)
    acc = jnp.zeros((2 * ROWS, wide), f32)
    for s in range(SESS):
        part = jnp.where(us2 == s, both, 0.0).astype(bf16)
        acc += jnp.dot(part, value_ref[s], preferred_element_type=f32)
    acc = jnp.where(mine, acc[:ROWS] + acc[ROWS:], 0.0)
    out = jnp.zeros((ROWS, HDIM), f32)
    new = jnp.zeros((ROWS, HDIM), f32)
    for k in range(heads):
        out += acc[:, k * HDIM : (k + 1) * HDIM]
        new += fresh[:, k * HDIM : (k + 1) * HDIM]
    out_ref[0] = out
    out_ref[1] = new
    lane = iota((ROWS, HDIM), 1)
    out_ref[2] = jnp.where(lane == 0, top, jnp.where(lane == 1, total, own * root))


def score_body(qx_ref, msg_ref, out_ref, code_ref):
    sources, cap, width = msg_ref.shape
    n = sources * cap
    blocks = qx_ref.shape[0] // 2
    heads = GROUP - 1
    q = qx_ref[...].astype(f32).reshape(blocks, 2, ROWS, 256)
    fold = jnp.concatenate([spare_row(q[:, k, :, 0:128], heads, 32) for k in range(2)], axis=-1)
    src = iota((256, 128), 0)
    unfold = ((src // 128) * 32 + src % 32 == iota((256, 128), 1)) & (src % 128 < heads * 32)
    odd = jnp.dot(
        fold.reshape(blocks * ROWS, 256).astype(bf16), unfold.astype(bf16), preferred_element_type=f32
    )
    even = jnp.concatenate([q[:, 0], q[:, 1]], axis=-1).reshape(blocks * ROWS, 512)
    a = jnp.concatenate([even.astype(bf16), odd.astype(bf16)], axis=-1)
    s = lax.dot_general(a, msg_ref[...].reshape(n, width), NT, preferred_element_type=f32)
    tail = msg_ref[:, :, width - 128 : width].reshape(n, 128)
    one = (iota((ROWS, 128), 1) == 64 + 48).astype(bf16)
    code = lax.dot_general(one, tail, NT, preferred_element_type=f32)
    code_ref[...] = code
    s = s.reshape(blocks, ROWS, n)
    out_ref[...] = jnp.where(code[None, 0:GROUP] == 2.0, s[:, GROUP:ROWS], s[:, 0:GROUP])


def soft_body(parts_ref, code_ref, cache_ref, out_ref, base_ref):
    heads = GROUP - 1
    n = code_ref.shape[1]
    root = 1.0 / math.sqrt(HDIM)
    s = jnp.sum(parts_ref[...], axis=0) * root
    s = jnp.concatenate([s, s], axis=0)
    u, h = rows_of((ROWS, n))
    seen = code_ref[...] == (1 + u).astype(f32)
    s = jnp.where(seen, s, LOW)
    stats = cache_ref[2]
    top_c, total_c, own = stats[:, 0:1], stats[:, 1:2], stats[:, 2:3]
    top = jnp.maximum(jnp.maximum(top_c, own), jnp.max(s, axis=1, keepdims=True))
    weight = jnp.where(seen, jnp.exp(s - top), 0.0)
    scale_c = jnp.exp(top_c - top)
    own_w = jnp.exp(own - top)
    den = jnp.sum(weight, axis=1, keepdims=True) + total_c * scale_c + own_w
    prob = jnp.where(h < heads, weight / den, 0.0)
    prob = prob[0:GROUP] + prob[GROUP:ROWS]
    out_ref[...] = jnp.broadcast_to(prob[None], out_ref.shape).astype(bf16)
    own_p = (own_w / den).astype(bf16).astype(f32)
    base_ref[...] = cache_ref[0] * (scale_c / den) + own_p * cache_ref[1]


def mix_body(prob_ref, code_ref, msg_ref, out_ref):
    sources, cap, width = msg_ref.shape
    n = sources * cap
    blocks = prob_ref.shape[0]
    heads = GROUP - 1
    p = prob_ref[...].astype(f32)
    u, _ = rows_of((ROWS, n))
    p = jnp.where((code_ref[...] == (1 + u).astype(f32))[None], jnp.concatenate([p, p], axis=1), 0.0)
    p = p.reshape(blocks * ROWS, n).astype(bf16)
    y = jnp.dot(p, msg_ref[...].reshape(n, width), preferred_element_type=f32)
    dst = iota((128, 256), 1)
    spread = ((iota((128, 256), 0) == dst % 64) & (dst < heads * 64)).astype(bf16)
    odd = jnp.dot(y[:, 512:640].astype(bf16), spread, preferred_element_type=f32)
    _, h = rows_of((blocks * ROWS, 256))
    odd = jnp.where(dst[0:1] // 64 == h, odd, 0.0).reshape(blocks, ROWS, 256)
    sums = [jnp.sum(odd[:, k : k + GROUP], axis=1, keepdims=True) for k in (0, GROUP)]
    u, h = rows_of((blocks, ROWS, 256))
    y = y.reshape(blocks, ROWS, width)
    first = jnp.where(h == heads, jnp.where(u == 0, sums[0], sums[1]), y[:, :, 0:256])
    out_ref[:, :, 0:256] = first.astype(bf16)
    out_ref[:, :, 256:512] = y[:, :, 256:512].astype(bf16)


def last_body(y_ref, w_ref, base_ref, out_ref, most_ref, rest_ref, most_sem, rest_sem):
    blocks = y_ref.shape[0]
    insts = 2 * blocks
    heads = out_ref.shape[1] // HDIM
    wide = heads * HDIM
    feats = w_ref.shape[0] // insts
    copies = []
    for a in range(insts):
        most = pltpu.make_async_copy(
            w_ref.at[pl.ds(a * feats, 256)], most_ref.at[pl.ds(a * 256, 256)], most_sem.at[a]
        )
        rest = pltpu.make_async_copy(
            w_ref.at[pl.ds(a * feats + 256, 32)], rest_ref.at[pl.ds(a * 32, 32)], rest_sem.at[a]
        )
        most.start()
        rest.start()
        copies.append((most, rest))
    y = y_ref[...].astype(f32)
    fold = spare_row(y[:, :, 0:256], heads, 64).reshape(blocks // 2, 2, ROWS, 256)
    fold = jnp.concatenate([fold[:, 0], fold[:, 1]], axis=-1).reshape(blocks // 2 * ROWS, 512)
    src = iota((512, 128), 0)
    unfold = ((src // 256) * 64 + src % 64 == iota((512, 128), 1)) & (src % 256 < heads * 64)
    odd = jnp.dot(fold.astype(bf16), unfold.astype(bf16), preferred_element_type=f32)
    odd = odd.reshape(blocks // 2, ROWS, 128)
    r = jnp.zeros((ROWS, wide), f32)
    step = 4
    for j in range(0, blocks, step):
        for most, rest in copies[2 * j : 2 * (j + step)]:
            most.wait()
            rest.wait()
        even = jnp.concatenate([y[k] for k in range(j, j + step)], axis=-1).astype(bf16)
        r += jnp.dot(even, most_ref[j * 512 : (j + step) * 512], preferred_element_type=f32)
        pair = jnp.concatenate([odd[k] for k in range(j // 2, (j + step) // 2)], axis=-1).astype(bf16)
        r += jnp.dot(pair, rest_ref[j * 64 : (j + step) * 64], preferred_element_type=f32)
    _, h = rows_of((ROWS, HDIM))
    t = base_ref[...]
    for k in range(heads):
        t += jnp.where(h == k, r[:, k * HDIM : (k + 1) * HDIM], 0.0)
    for k in range(heads):
        both = jnp.concatenate([t[k : k + 1], t[GROUP + k : GROUP + k + 1]], axis=0)
        out_ref[:, k * HDIM : (k + 1) * HDIM] = both.astype(bf16)


def local(
    hidden_rows,
    send_counts,
    row_session,
    row_position,
    resident_lengths,
    kv_weight,
    key_cache,
    value_cache,
    query,
    new_key,
    new_value,
):
    _, insts, cap, feats = hidden_rows.shape
    wide = query.shape[1]
    slots = insts * cap
    blocks = lax.axis_size("head")
    width = feats + 64
    swap = lambda t, axis: lax.all_to_all(t, axis, split_axis=0, concat_axis=0, tiled=True)

    values = jnp.concatenate([kv_weight[:, k + HDIM : k + 2 * HDIM] for k in range(0, 2 * wide, 2 * HDIM)], axis=1)
    values = lax.all_gather(values, "inst", axis=0, tiled=True)

    msg = pl.pallas_call(
        pack_body,
        out_shape=jax.ShapeDtypeStruct((insts, cap, width), bf16),
        in_specs=vmem(4),
        out_specs=vmem(1)[0],
    )(hidden_rows[0], query, send_counts, row_session[0].T)
    msg = swap(msg, "inst")

    cache = pl.pallas_call(
        cache_body,
        grid=(1,),
        out_shape=jax.ShapeDtypeStruct((3, ROWS, HDIM), f32),
        in_specs=[pl.BlockSpec(memory_space=pltpu.SMEM)]
        + vmem(3)
        + [pl.BlockSpec((SESS, RES_MAX, wide), lambda i: (0, 0, 0))] * 2,
        out_specs=vmem(1)[0],
    )(resident_lengths, query, new_key, new_value, key_cache, value_cache)

    qw = pl.pallas_call(
        qw_body,
        grid=(1,),
        out_shape=jax.ShapeDtypeStruct((insts, ROWS, 256), bf16),
        in_specs=[pl.BlockSpec((insts, cap, 128), lambda i: (0, 0, width // 128 - 1)), vmem(1)[0]],
        out_specs=vmem(1)[0],
        scratch_shapes=[pltpu.VMEM((128, wide), bf16)],
    )(msg, kv_weight)
    qx = swap(swap(qw, "inst"), "head")

    part, code = pl.pallas_call(
        score_body,
        out_shape=(
            jax.ShapeDtypeStruct((blocks, GROUP, slots), f32),
            jax.ShapeDtypeStruct((ROWS, slots), f32),
        ),
        in_specs=vmem(2),
        out_specs=tuple(vmem(2)),
    )(qx, msg)
    part = swap(part, "head")

    prob, base = pl.pallas_call(
        soft_body,
        out_shape=(
            jax.ShapeDtypeStruct((blocks, GROUP, slots), bf16),
            jax.ShapeDtypeStruct((ROWS, HDIM), f32),
        ),
        in_specs=vmem(3),
        out_specs=tuple(vmem(2)),
    )(part, code, cache)
    prob = swap(prob, "head")

    y = pl.pallas_call(
        mix_body,
        out_shape=jax.ShapeDtypeStruct((blocks, ROWS, 512), bf16),
        in_specs=vmem(3),
        out_specs=vmem(1)[0],
    )(prob, code, msg)
    y = swap(y, "head")

    return pl.pallas_call(
        last_body,
        out_shape=jax.ShapeDtypeStruct((SESS, wide), bf16),
        in_specs=[vmem(1)[0], pl.BlockSpec(memory_space=pl.ANY), vmem(1)[0]],
        out_specs=vmem(1)[0],
        scratch_shapes=[
            pltpu.VMEM((insts * 256, wide), bf16),
            pltpu.VMEM((insts * 32, wide), bf16),
            pltpu.SemaphoreType.DMA((insts,)),
            pltpu.SemaphoreType.DMA((insts,)),
        ],
        compiler_params=pltpu.CompilerParams(vmem_limit_bytes=56 * 2**20),
    )(y, values, base)


def solution(mesh):
    placed = (
        P("inst", None, None, "head"),
        P("inst", None),
        P("inst", None, None),
        P("inst", None, None),
        P("inst"),
        P("inst", "head"),
        P("inst", None, "head"),
        P("inst", None, "head"),
        P("inst", "head"),
        P("inst", "head"),
        P("inst", "head"),
    )
    return jax.shard_map(
        local, mesh=mesh, in_specs=placed, out_specs=P("inst", "head"), check_vma=False
    )
```

```python
import math

import jax
import jax.numpy as jnp
from jax import lax
from jax.experimental import pallas as pl
from jax.experimental.pallas import tpu as pltpu
from jax.sharding import PartitionSpec as P

HDIM = 128
SESS = 2
RES_MAX = 512
ROWS = 8
GROUP = 4
LOW = -1e30
f32 = jnp.float32
bf16 = jnp.bfloat16
NT = (((1,), (1,)), ((), ()))


def iota(shape, dim):
    return lax.broadcasted_iota(jnp.int32, shape, dim)


def rows_of(shape):
    row = iota(shape, len(shape) - 2) % ROWS
    return row // GROUP, row % GROUP


def spare_row(t, heads, part):
    u, h = rows_of(t.shape)
    own = jnp.where(u == 0, t[..., heads : heads + 1, :], t[..., GROUP + heads : GROUP + heads + 1, :])
    return jnp.where(iota(t.shape, t.ndim - 1) // part == h, own, 0.0)


def vmem(n):
    return [pl.BlockSpec(memory_space=pltpu.VMEM)] * n


MAIN = (((0, 256),), ((224, 64), (32, 64), (96, 128)))
ODD = (256, 0)


def pack_body(x_ref, tail_ref, q_ref, counts_ref, session_ref, w_ref, out_ref, values_ref, new_ref, sem, w_sem):
    dests, cap, feats = x_ref.shape
    heads = q_ref.shape[1] // HDIM
    wide = heads * HDIM
    odd = lax.axis_index("inst") % 2

    def moves(parity):
        out = []
        at = 0
        for start, size in MAIN[parity] + ((ODD[parity], 32),):
            for h in range(heads):
                out.append(
                    pltpu.make_async_copy(
                        w_ref.at[pl.ds(start, size), pl.ds((2 * h + 1) * HDIM, HDIM)],
                        values_ref.at[pl.ds(at, size), pl.ds(h * HDIM, HDIM)],
                        w_sem.at[len(out)],
                    )
                )
            at += size
        return out

    for parity in range(2):

        @pl.when(odd == parity)
        def _():
            for move in moves(parity):
                move.start()

    rows = pltpu.make_async_copy(x_ref.at[:, :, pl.ds(0, 512)], out_ref.at[:, :, pl.ds(0, 512)], sem.at[0])
    rows.start()
    q = q_ref[...].astype(f32)
    row = iota((cap, wide), 0)
    lane = iota((cap, wide), 1)
    spread = jnp.where(row < 8, q[0:1], q[1:2])
    spread = jnp.where((lane % HDIM) // 16 == row % 8, spread, 0.0)
    src = iota((wide, 128), 0)
    dst = iota((wide, 128), 1) - 64
    fold = ((src // HDIM) * 16 + src % 16 == dst).astype(bf16)
    ext = jnp.dot(spread.astype(bf16), fold, preferred_element_type=f32)
    live = iota((cap, dests), 0) < counts_ref[...]
    code = jnp.where(live, 1 + session_ref[...], 0).astype(f32)
    lane = iota((cap, 128), 1)
    for i in range(dests):
        t = jnp.where(lane == 64 + 48, code[:, i : i + 1], ext)
        new_ref[i] = jnp.where(lane < 64, tail_ref[i].astype(f32), t).astype(bf16)
    tail = pltpu.make_async_copy(new_ref, out_ref.at[:, :, pl.ds(512, 128)], sem.at[1])
    tail.start()
    for parity in range(2):

        @pl.when(odd == parity)
        def _():
            for move in moves(parity):
                move.wait()

    rows.wait()
    tail.wait()


def qw_body(msg_ref, w_ref, _, out_ref, main_ref, odd_ref, tail_ref, sem):
    sources, cap, width = msg_ref.shape
    fetch = pltpu.make_async_copy(msg_ref.at[:, :, pl.ds(width - 128, 128)], tail_ref, sem)
    fetch.start()
    heads = w_ref.shape[1] // (2 * HDIM)
    wide = heads * HDIM
    parity = lax.axis_index("inst") % 2
    odd_ref[...] = jnp.zeros_like(odd_ref)
    for p in range(2):

        @pl.when(parity == p)
        def _():
            for h in range(heads):
                mine = slice(h * HDIM, (h + 1) * HDIM)
                keys = slice(2 * h * HDIM, (2 * h + 1) * HDIM)
                at = 0
                for start, size in MAIN[p]:
                    main_ref[at : at + size, mine] = w_ref[start : start + size, keys]
                    at += size
                odd_ref[h * 32 : h * 32 + 32, mine] = w_ref[ODD[p] : ODD[p] + 32, keys]

    n = sources * cap
    fetch.wait()
    tail = tail_ref[...].reshape(n, 128)
    src = iota((128, wide), 0) - 64
    dst = iota((128, wide), 1)
    unfold = ((dst // HDIM) * 16 + dst % 16 == src).astype(bf16)
    z = jnp.dot(tail, unfold, preferred_element_type=f32)
    z = jnp.where((iota((n, wide), 1) % HDIM) // 16 == iota((n, wide), 0) % 8, z, 0.0).astype(bf16)
    m = sources * ROWS
    take = (iota((m, n), 0) // GROUP == iota((m, n), 1) // 8).astype(bf16)
    queries = jnp.dot(take, z, preferred_element_type=f32)
    _, h = rows_of((m, wide))
    queries = jnp.where((iota((m, wide), 1) // HDIM == h) | (h == heads), queries, 0.0).astype(bf16)
    even = lax.dot_general(queries, main_ref[...], NT, preferred_element_type=f32)
    odd = lax.dot_general(queries, odd_ref[...], NT, preferred_element_type=f32)
    _, h = rows_of((m, 128))
    first = jnp.where(h == heads, odd, even[:, 0:128])
    out_ref[:, :, 0:128] = first.reshape(sources, ROWS, 128).astype(bf16)
    out_ref[:, :, 128:256] = even[:, 128:256].reshape(sources, ROWS, 128).astype(bf16)


def cache_body(lengths_ref, q_ref, nk_ref, nv_ref, key_ref, value_ref, out_ref):
    heads = q_ref.shape[1] // HDIM
    wide = heads * HDIM
    span = key_ref.shape[1]
    root = 1.0 / math.sqrt(HDIM)
    u, h = rows_of((ROWS, wide))
    mine = iota((ROWS, wide), 1) // HDIM == h
    q = q_ref[...].astype(f32)
    nk = nk_ref[...].astype(f32)
    nv = nv_ref[...].astype(f32)
    scores = jnp.zeros((ROWS, span), f32)
    own = jnp.zeros((ROWS, 1), f32)
    fresh = jnp.zeros((ROWS, wide), f32)
    for s in range(SESS):
        here = mine & (u == s)
        qs = jnp.where(here, q[s : s + 1], 0.0)
        scores += lax.dot_general(qs.astype(bf16), key_ref[s], NT, preferred_element_type=f32)
        own += jnp.sum(qs * nk[s : s + 1], axis=1, keepdims=True)
        fresh += jnp.where(here, nv[s : s + 1], 0.0)
    scores = scores * root
    us, _ = rows_of((ROWS, span))
    length = jnp.where(us == 0, lengths_ref[0], lengths_ref[1])
    seen = iota((ROWS, span), 1) < length
    scores = jnp.where(seen, scores, LOW)
    top = jnp.max(scores, axis=1, keepdims=True)
    weight = jnp.where(seen, jnp.exp(scores - top), 0.0)
    total = jnp.sum(weight, axis=1, keepdims=True)
    high = weight.astype(bf16).astype(f32)
    both = jnp.concatenate([high, weight - high], axis=0)
    us2 = jnp.concatenate([us, us], axis=0)
    acc = jnp.zeros((2 * ROWS, wide), f32)
    for s in range(SESS):
        part = jnp.where(us2 == s, both, 0.0).astype(bf16)
        acc += jnp.dot(part, value_ref[s], preferred_element_type=f32)
    acc = jnp.where(mine, acc[:ROWS] + acc[ROWS:], 0.0)
    out = jnp.zeros((ROWS, HDIM), f32)
    new = jnp.zeros((ROWS, HDIM), f32)
    for k in range(heads):
        out += acc[:, k * HDIM : (k + 1) * HDIM]
        new += fresh[:, k * HDIM : (k + 1) * HDIM]
    out_ref[0] = out
    out_ref[1] = new
    lane = iota((ROWS, HDIM), 1)
    out_ref[2] = jnp.where(lane == 0, top, jnp.where(lane == 1, total, own * root))


def score_body(qx_ref, msg_ref, out_ref, code_ref, x_ref, sem):
    sources, cap, width = msg_ref.shape
    fetch = pltpu.make_async_copy(msg_ref, x_ref, sem)
    fetch.start()
    n = sources * cap
    blocks = qx_ref.shape[0] // 2
    heads = GROUP - 1
    q = qx_ref[...].astype(f32).reshape(blocks, 2, ROWS, 256)
    fold = jnp.concatenate([spare_row(q[:, k, :, 0:128], heads, 32) for k in range(2)], axis=-1)
    src = iota((256, 128), 0)
    unfold = ((src // 128) * 32 + src % 32 == iota((256, 128), 1)) & (src % 128 < heads * 32)
    odd = jnp.dot(
        fold.reshape(blocks * ROWS, 256).astype(bf16), unfold.astype(bf16), preferred_element_type=f32
    )
    even = q[:, 0].reshape(blocks * ROWS, 256)
    other = q[:, 1].reshape(blocks * ROWS, 256)
    low = iota(odd.shape, 1) < 64
    tiles = [even, jnp.where(low, odd, other[:, 0:128]), other[:, 128:256], jnp.where(low, other[:, 0:128], 0.0)]
    a = jnp.concatenate([t.astype(bf16) for t in tiles], axis=-1)
    one = (iota((ROWS, 128), 1) == 64 + 48).astype(bf16)
    fetch.wait()
    s = lax.dot_general(a, x_ref[...].reshape(n, width), NT, preferred_element_type=f32)
    tail = x_ref[:, :, width - 128 : width].reshape(n, 128)
    code = lax.dot_general(one, tail, NT, preferred_element_type=f32)
    code_ref[...] = code
    s = s.reshape(blocks, ROWS, n)
    out_ref[...] = jnp.where(code[None, 0:GROUP] == 2.0, s[:, GROUP:ROWS], s[:, 0:GROUP])


def soft_body(parts_ref, code_ref, cache_ref, out_ref, base_ref, here_ref, sem):
    fetch = pltpu.make_async_copy(parts_ref, here_ref, sem)
    fetch.start()
    heads = GROUP - 1
    n = code_ref.shape[1]
    root = 1.0 / math.sqrt(HDIM)
    fetch.wait()
    s = jnp.sum(here_ref[...], axis=0) * root
    s = jnp.concatenate([s, s], axis=0)
    u, h = rows_of((ROWS, n))
    seen = code_ref[...] == (1 + u).astype(f32)
    s = jnp.where(seen, s, LOW)
    stats = cache_ref[2]
    top_c, total_c, own = stats[:, 0:1], stats[:, 1:2], stats[:, 2:3]
    top = jnp.maximum(jnp.maximum(top_c, own), jnp.max(s, axis=1, keepdims=True))
    weight = jnp.where(seen, jnp.exp(s - top), 0.0)
    scale_c = jnp.exp(top_c - top)
    own_w = jnp.exp(own - top)
    den = jnp.sum(weight, axis=1, keepdims=True) + total_c * scale_c + own_w
    prob = jnp.where(h < heads, weight / den, 0.0)
    prob = prob[0:GROUP] + prob[GROUP:ROWS]
    out_ref[...] = jnp.broadcast_to(prob[None], out_ref.shape).astype(bf16)
    own_p = (own_w / den).astype(bf16).astype(f32)
    base_ref[...] = cache_ref[0] * (scale_c / den) + own_p * cache_ref[1]


def mix_body(prob_ref, code_ref, msg_ref, out_ref, x_ref, sem):
    sources, cap, width = msg_ref.shape
    fetch = pltpu.make_async_copy(msg_ref, x_ref, sem)
    fetch.start()
    n = sources * cap
    blocks = prob_ref.shape[0]
    heads = GROUP - 1
    p = prob_ref[...].astype(f32)
    u, _ = rows_of((ROWS, n))
    p = jnp.where((code_ref[...] == (1 + u).astype(f32))[None], jnp.concatenate([p, p], axis=1), 0.0)
    p = p.reshape(blocks * ROWS, n).astype(bf16)
    fetch.wait()
    y = jnp.dot(p, x_ref[...].reshape(n, width), preferred_element_type=f32)
    dst = iota((128, 256), 1)
    spread = ((iota((128, 256), 0) == dst % 64) & (dst < heads * 64)).astype(bf16)
    odd = jnp.dot(y[:, 256:384].astype(bf16), spread, preferred_element_type=f32)
    _, h = rows_of((blocks * ROWS, 256))
    odd = jnp.where(dst[0:1] // 64 == h, odd, 0.0).reshape(blocks, ROWS, 256)
    sums = [jnp.sum(odd[:, k : k + GROUP], axis=1, keepdims=True) for k in (0, GROUP)]
    u, h = rows_of((blocks, ROWS, 256))
    y = y.reshape(blocks, ROWS, width)
    first = jnp.where(h == heads, jnp.where(u == 0, sums[0], sums[1]), y[:, :, 0:256])
    out_ref[:, :, 0:256] = first.astype(bf16)
    low = iota((blocks, ROWS, 128), 2) < 64
    out_ref[:, :, 256:384] = jnp.where(low, y[:, :, 512:640], y[:, :, 256:384]).astype(bf16)
    out_ref[:, :, 384:512] = y[:, :, 384:512].astype(bf16)


def last_body(y_ref, w_ref, base_ref, out_ref, most_ref, rest_ref, most_sem, rest_sem):
    blocks = y_ref.shape[0]
    insts = 2 * blocks
    heads = out_ref.shape[1] // HDIM
    wide = heads * HDIM
    feats = w_ref.shape[0] // insts
    copies = []
    for a in range(insts):
        most = pltpu.make_async_copy(
            w_ref.at[pl.ds(a * feats, 256)], most_ref.at[pl.ds(a * 256, 256)], most_sem.at[a]
        )
        rest = pltpu.make_async_copy(
            w_ref.at[pl.ds(a * feats + 256, 32)], rest_ref.at[pl.ds(a * 32, 32)], rest_sem.at[a]
        )
        most.start()
        rest.start()
        copies.append((most, rest))
    y = y_ref[...].astype(f32)
    fold = spare_row(y[:, :, 0:256], heads, 64).reshape(blocks // 2, 2, ROWS, 256)
    fold = jnp.concatenate([fold[:, 0], fold[:, 1]], axis=-1).reshape(blocks // 2 * ROWS, 512)
    src = iota((512, 128), 0)
    unfold = ((src // 256) * 64 + src % 64 == iota((512, 128), 1)) & (src % 256 < heads * 64)
    odd = jnp.dot(fold.astype(bf16), unfold.astype(bf16), preferred_element_type=f32)
    odd = odd.reshape(blocks // 2, ROWS, 128)
    extra = jnp.zeros((2 * ROWS, 256), f32)

    def add(left, ref, at, half):
        first, second = left[:, 0:half], left[:, half : 2 * half]
        both = jnp.concatenate([first, second], axis=0).astype(bf16)
        one = jnp.dot(left.astype(bf16), ref[at : at + 2 * half, 0:256], preferred_element_type=f32)
        pair = jnp.concatenate([ref[at : at + half, 256:384], ref[at + half : at + 2 * half, 256:384]], axis=1)
        return one, jnp.dot(both, pair, preferred_element_type=f32)

    r = jnp.zeros((ROWS, 256), f32)
    step = 4
    for j in range(0, blocks, step):
        for most, rest in copies[2 * j : 2 * (j + step)]:
            most.wait()
            rest.wait()
        even = jnp.concatenate([y[k] for k in range(j, j + step)], axis=-1)
        pair = jnp.concatenate([odd[k] for k in range(j // 2, (j + step) // 2)], axis=-1)
        for left, ref, at in ((even, most_ref, j * 512), (pair, rest_ref, j * 64)):
            one, two = add(left, ref, at, left.shape[1] // 2)
            r += one
            extra += two
    r = jnp.concatenate([r, extra[0:ROWS, 0:128] + extra[ROWS : 2 * ROWS, 128:256]], axis=1)
    _, h = rows_of((ROWS, HDIM))
    t = base_ref[...]
    for k in range(heads):
        t += jnp.where(h == k, r[:, k * HDIM : (k + 1) * HDIM], 0.0)
    for k in range(heads):
        both = jnp.concatenate([t[k : k + 1], t[GROUP + k : GROUP + k + 1]], axis=0)
        out_ref[:, k * HDIM : (k + 1) * HDIM] = both.astype(bf16)


def local(
    hidden_rows,
    send_counts,
    row_session,
    row_position,
    resident_lengths,
    kv_weight,
    key_cache,
    value_cache,
    query,
    new_key,
    new_value,
):
    _, insts, cap, feats = hidden_rows.shape
    wide = query.shape[1]
    slots = insts * cap
    blocks = lax.axis_size("head")
    width = feats + 64
    swap = lambda t, axis: lax.all_to_all(t, axis, split_axis=0, concat_axis=0, tiled=True)

    anywhere = pl.BlockSpec(memory_space=pl.ANY)
    msg, values = pl.pallas_call(
        pack_body,
        grid=(1,),
        out_shape=(
            jax.ShapeDtypeStruct((insts, cap, width), bf16),
            jax.ShapeDtypeStruct((kv_weight.shape[0], wide), bf16),
        ),
        in_specs=[anywhere, pl.BlockSpec((insts, cap, 128), lambda i: (0, 0, 4))] + vmem(3) + [anywhere],
        out_specs=(anywhere, anywhere),
        scratch_shapes=[
            pltpu.VMEM((insts, cap, 128), bf16),
            pltpu.SemaphoreType.DMA((2,)),
            pltpu.SemaphoreType.DMA((4 * wide // HDIM,)),
        ],
    )(hidden_rows[0], hidden_rows[0], query, send_counts, row_session[0].T, kv_weight)
    values = lax.all_gather(values, "inst", axis=0, tiled=True)
    msg = swap(msg, "inst")

    cache = pl.pallas_call(
        cache_body,
        grid=(1,),
        out_shape=jax.ShapeDtypeStruct((3, ROWS, HDIM), f32),
        in_specs=[pl.BlockSpec(memory_space=pltpu.SMEM)]
        + vmem(3)
        + [pl.BlockSpec((SESS, RES_MAX, wide), lambda i: (0, 0, 0))] * 2,
        out_specs=vmem(1)[0],
    )(resident_lengths, query, new_key, new_value, key_cache, value_cache)

    qw = pl.pallas_call(
        qw_body,
        out_shape=jax.ShapeDtypeStruct((insts, ROWS, 256), bf16),
        in_specs=[anywhere, vmem(1)[0], anywhere],
        out_specs=vmem(1)[0],
        scratch_shapes=[
            pltpu.VMEM((256, wide), bf16),
            pltpu.VMEM((128, wide), bf16),
            pltpu.VMEM((insts, cap, 128), bf16),
            pltpu.SemaphoreType.DMA,
        ],
    )(msg, kv_weight, cache)
    qx = swap(swap(qw, "inst"), "head")

    part, code = pl.pallas_call(
        score_body,
        out_shape=(
            jax.ShapeDtypeStruct((blocks, GROUP, slots), f32),
            jax.ShapeDtypeStruct((ROWS, slots), f32),
        ),
        in_specs=[vmem(1)[0], anywhere],
        out_specs=tuple(vmem(2)),
        scratch_shapes=[pltpu.VMEM((insts, cap, width), bf16), pltpu.SemaphoreType.DMA],
    )(qx, msg)
    part = swap(part, "head")

    prob, base = pl.pallas_call(
        soft_body,
        out_shape=(
            jax.ShapeDtypeStruct((blocks, GROUP, slots), bf16),
            jax.ShapeDtypeStruct((ROWS, HDIM), f32),
        ),
        in_specs=[anywhere] + vmem(2),
        out_specs=tuple(vmem(2)),
        scratch_shapes=[pltpu.VMEM((blocks, GROUP, slots), f32), pltpu.SemaphoreType.DMA],
    )(part, code, cache)
    prob = swap(prob, "head")

    y = pl.pallas_call(
        mix_body,
        out_shape=jax.ShapeDtypeStruct((blocks, ROWS, 512), bf16),
        in_specs=vmem(2) + [anywhere],
        out_specs=vmem(1)[0],
        scratch_shapes=[pltpu.VMEM((insts, cap, width), bf16), pltpu.SemaphoreType.DMA],
    )(prob, code, msg)
    y = swap(y, "head")

    return pl.pallas_call(
        last_body,
        out_shape=jax.ShapeDtypeStruct((SESS, wide), bf16),
        in_specs=[vmem(1)[0], pl.BlockSpec(memory_space=pl.ANY), vmem(1)[0]],
        out_specs=vmem(1)[0],
        scratch_shapes=[
            pltpu.VMEM((insts * 256, wide), bf16),
            pltpu.VMEM((insts * 32, wide), bf16),
            pltpu.SemaphoreType.DMA((insts,)),
            pltpu.SemaphoreType.DMA((insts,)),
        ],
        compiler_params=pltpu.CompilerParams(vmem_limit_bytes=56 * 2**20),
    )(y, values, base)


def solution(mesh):
    placed = (
        P("inst", None, None, "head"),
        P("inst", None),
        P("inst", None, None),
        P("inst", None, None),
        P("inst"),
        P("inst", "head"),
        P("inst", None, "head"),
        P("inst", None, "head"),
        P("inst", "head"),
        P("inst", "head"),
        P("inst", "head"),
    )
    return jax.shard_map(
        local, mesh=mesh, in_specs=placed, out_specs=P("inst", "head"), check_vma=False
    )
```

```python
import math

import jax
import jax.numpy as jnp
from jax import lax
from jax.experimental import pallas as pl
from jax.experimental.pallas import tpu as pltpu
from jax.sharding import PartitionSpec as P

HDIM = 128
SESS = 2
RES_MAX = 512
ROWS = 8
GROUP = 4
LOW = -1e30
f32 = jnp.float32
bf16 = jnp.bfloat16
NT = (((1,), (1,)), ((), ()))


def iota(shape, dim):
    return lax.broadcasted_iota(jnp.int32, shape, dim)


def rows_of(shape):
    row = iota(shape, len(shape) - 2) % ROWS
    return row // GROUP, row % GROUP


def spare_row(t, heads, part):
    u, h = rows_of(t.shape)
    own = jnp.where(u == 0, t[..., heads : heads + 1, :], t[..., GROUP + heads : GROUP + heads + 1, :])
    return jnp.where(iota(t.shape, t.ndim - 1) // part == h, own, 0.0)


def vmem(n):
    return [pl.BlockSpec(memory_space=pltpu.VMEM)] * n


def pack_body(x_ref, q_ref, counts_ref, session_ref, w_ref, out_ref, values_ref):
    dests, cap, feats = x_ref.shape
    heads = q_ref.shape[1] // HDIM
    wide = heads * HDIM
    for h in range(heads):
        values_ref[:, h * HDIM : (h + 1) * HDIM] = w_ref[:, (2 * h + 1) * HDIM : (2 * h + 2) * HDIM]
    out_ref[:, :, 0:256] = x_ref[:, :, 0:256]
    out_ref[:, :, 256:512] = x_ref[:, :, 288:544]
    q = q_ref[...].astype(f32)
    row = iota((cap, wide), 0)
    lane = iota((cap, wide), 1)
    spread = jnp.where(row < 8, q[0:1], q[1:2])
    spread = jnp.where((lane % HDIM) // 16 == row % 8, spread, 0.0)
    src = iota((wide, 128), 0)
    dst = iota((wide, 128), 1) - 64
    fold = ((src // HDIM) * 16 + src % 16 == dst).astype(bf16)
    ext = jnp.dot(spread.astype(bf16), fold, preferred_element_type=f32)
    live = iota((cap, dests), 0) < counts_ref[...]
    code = jnp.where(live, 1 + session_ref[...], 0).astype(f32)
    lane = iota((cap, 128), 1)
    none = jnp.zeros((cap, 128 - (feats - 512)), f32)
    for i in range(dests):
        low = x_ref[i, :, 256:384].astype(f32)
        high = jnp.concatenate([x_ref[i, :, 512:feats].astype(f32), none], axis=1)
        t = jnp.where(lane == 64 + 48, code[:, i : i + 1], ext)
        t = jnp.where(lane < 32, low, jnp.where(lane < 64, high, t))
        out_ref[i, :, 512:640] = t.astype(bf16)


def qw_body(msg_ref, w_ref, out_ref, odd_ref):
    sources, cap, _ = msg_ref.shape
    heads = w_ref.shape[1] // (2 * HDIM)
    wide = heads * HDIM
    odd_ref[...] = jnp.zeros_like(odd_ref)
    for h in range(heads):
        odd_ref[h * 32 : h * 32 + 32, h * HDIM : (h + 1) * HDIM] = w_ref[256:288, 2 * h * HDIM : (2 * h + 1) * HDIM]
    keys = jnp.concatenate([w_ref[0:256, 2 * h * HDIM : (2 * h + 1) * HDIM] for h in range(heads)], axis=1)

    n = sources * cap
    tail = msg_ref[...].reshape(n, 128)
    src = iota((128, wide), 0) - 64
    dst = iota((128, wide), 1)
    unfold = ((dst // HDIM) * 16 + dst % 16 == src).astype(bf16)
    z = jnp.dot(tail, unfold, preferred_element_type=f32)
    z = jnp.where((iota((n, wide), 1) % HDIM) // 16 == iota((n, wide), 0) % 8, z, 0.0).astype(bf16)
    m = sources * ROWS
    take = (iota((m, n), 0) // GROUP == iota((m, n), 1) // 8).astype(bf16)
    queries = jnp.dot(take, z, preferred_element_type=f32)
    _, h = rows_of((m, wide))
    queries = jnp.where((iota((m, wide), 1) // HDIM == h) | (h == heads), queries, 0.0).astype(bf16)
    even = lax.dot_general(queries, keys, NT, preferred_element_type=f32)
    odd = lax.dot_general(queries, odd_ref[...], NT, preferred_element_type=f32)
    _, h = rows_of((m, 128))
    first = jnp.where(h == heads, odd, even[:, 0:128])
    out_ref[:, :, 0:128] = first.reshape(sources, ROWS, 128).astype(bf16)
    out_ref[:, :, 128:256] = even[:, 128:256].reshape(sources, ROWS, 128).astype(bf16)


def cache_body(lengths_ref, q_ref, nk_ref, nv_ref, key_ref, value_ref, out_ref):
    heads = q_ref.shape[1] // HDIM
    wide = heads * HDIM
    span = key_ref.shape[1]
    root = 1.0 / math.sqrt(HDIM)
    u, h = rows_of((ROWS, wide))
    mine = iota((ROWS, wide), 1) // HDIM == h
    q = q_ref[...].astype(f32)
    nk = nk_ref[...].astype(f32)
    nv = nv_ref[...].astype(f32)
    scores = jnp.zeros((ROWS, span), f32)
    own = jnp.zeros((ROWS, 1), f32)
    fresh = jnp.zeros((ROWS, wide), f32)
    for s in range(SESS):
        here = mine & (u == s)
        qs = jnp.where(here, q[s : s + 1], 0.0)
        scores += lax.dot_general(qs.astype(bf16), key_ref[s], NT, preferred_element_type=f32)
        own += jnp.sum(qs * nk[s : s + 1], axis=1, keepdims=True)
        fresh += jnp.where(here, nv[s : s + 1], 0.0)
    scores = scores * root
    us, _ = rows_of((ROWS, span))
    length = jnp.where(us == 0, lengths_ref[0], lengths_ref[1])
    seen = iota((ROWS, span), 1) < length
    scores = jnp.where(seen, scores, LOW)
    top = jnp.max(scores, axis=1, keepdims=True)
    weight = jnp.where(seen, jnp.exp(scores - top), 0.0)
    total = jnp.sum(weight, axis=1, keepdims=True)
    high = weight.astype(bf16).astype(f32)
    both = jnp.concatenate([high, weight - high], axis=0)
    us2 = jnp.concatenate([us, us], axis=0)
    acc = jnp.zeros((2 * ROWS, wide), f32)
    for s in range(SESS):
        part = jnp.where(us2 == s, both, 0.0).astype(bf16)
        acc += jnp.dot(part, value_ref[s], preferred_element_type=f32)
    acc = jnp.where(mine, acc[:ROWS] + acc[ROWS:], 0.0)
    out = jnp.zeros((ROWS, HDIM), f32)
    new = jnp.zeros((ROWS, HDIM), f32)
    for k in range(heads):
        out += acc[:, k * HDIM : (k + 1) * HDIM]
        new += fresh[:, k * HDIM : (k + 1) * HDIM]
    out_ref[0] = out
    out_ref[1] = new
    lane = iota((ROWS, HDIM), 1)
    out_ref[2] = jnp.where(lane == 0, top, jnp.where(lane == 1, total, own * root))


def score_body(qx_ref, msg_ref, out_ref, code_ref):
    sources, cap, width = msg_ref.shape
    n = sources * cap
    blocks = qx_ref.shape[0] // 2
    heads = GROUP - 1
    q = qx_ref[...].astype(f32).reshape(blocks, 2, ROWS, 256)
    fold = jnp.concatenate([spare_row(q[:, k, :, 0:128], heads, 32) for k in range(2)], axis=-1)
    src = iota((256, 128), 0)
    unfold = ((src // 128) * 32 + src % 32 == iota((256, 128), 1)) & (src % 128 < heads * 32)
    odd = jnp.dot(
        fold.reshape(blocks * ROWS, 256).astype(bf16), unfold.astype(bf16), preferred_element_type=f32
    )
    even = jnp.concatenate([q[:, 0], q[:, 1]], axis=-1).reshape(blocks * ROWS, 512)
    a = jnp.concatenate([even.astype(bf16), odd.astype(bf16)], axis=-1)
    s = lax.dot_general(a, msg_ref[...].reshape(n, width), NT, preferred_element_type=f32)
    tail = msg_ref[:, :, width - 128 : width].reshape(n, 128)
    one = (iota((ROWS, 128), 1) == 64 + 48).astype(bf16)
    code = lax.dot_general(one, tail, NT, preferred_element_type=f32)
    code_ref[...] = code
    s = s.reshape(blocks, ROWS, n)
    out_ref[...] = jnp.where(code[None, 0:GROUP] == 2.0, s[:, GROUP:ROWS], s[:, 0:GROUP])


def soft_body(parts_ref, code_ref, cache_ref, out_ref, base_ref):
    heads = GROUP - 1
    n = code_ref.shape[1]
    root = 1.0 / math.sqrt(HDIM)
    s = jnp.sum(parts_ref[...], axis=0) * root
    s = jnp.concatenate([s, s], axis=0)
    u, h = rows_of((ROWS, n))
    seen = code_ref[...] == (1 + u).astype(f32)
    s = jnp.where(seen, s, LOW)
    stats = cache_ref[2]
    top_c, total_c, own = stats[:, 0:1], stats[:, 1:2], stats[:, 2:3]
    top = jnp.maximum(jnp.maximum(top_c, own), jnp.max(s, axis=1, keepdims=True))
    weight = jnp.where(seen, jnp.exp(s - top), 0.0)
    scale_c = jnp.exp(top_c - top)
    own_w = jnp.exp(own - top)
    den = jnp.sum(weight, axis=1, keepdims=True) + total_c * scale_c + own_w
    prob = jnp.where(h < heads, weight / den, 0.0)
    prob = prob[0:GROUP] + prob[GROUP:ROWS]
    out_ref[...] = jnp.broadcast_to(prob[None], out_ref.shape).astype(bf16)
    own_p = (own_w / den).astype(bf16).astype(f32)
    base_ref[...] = cache_ref[0] * (scale_c / den) + own_p * cache_ref[1]


def mix_body(prob_ref, code_ref, msg_ref, out_ref):
    sources, cap, width = msg_ref.shape
    n = sources * cap
    blocks = prob_ref.shape[0]
    heads = GROUP - 1
    p = prob_ref[...].astype(f32)
    u, _ = rows_of((ROWS, n))
    p = jnp.where((code_ref[...] == (1 + u).astype(f32))[None], jnp.concatenate([p, p], axis=1), 0.0)
    p = p.reshape(blocks * ROWS, n).astype(bf16)
    y = jnp.dot(p, msg_ref[...].reshape(n, width), preferred_element_type=f32)
    dst = iota((128, 256), 1)
    spread = ((iota((128, 256), 0) == dst % 64) & (dst < heads * 64)).astype(bf16)
    odd = jnp.dot(y[:, 512:640].astype(bf16), spread, preferred_element_type=f32)
    _, h = rows_of((blocks * ROWS, 256))
    odd = jnp.where(dst[0:1] // 64 == h, odd, 0.0).reshape(blocks, ROWS, 256)
    sums = [jnp.sum(odd[:, k : k + GROUP], axis=1, keepdims=True) for k in (0, GROUP)]
    u, h = rows_of((blocks, ROWS, 256))
    y = y.reshape(blocks, ROWS, width)
    first = jnp.where(h == heads, jnp.where(u == 0, sums[0], sums[1]), y[:, :, 0:256])
    out_ref[:, :, 0:256] = first.astype(bf16)
    out_ref[:, :, 256:512] = y[:, :, 256:512].astype(bf16)


def last_body(y_ref, w_ref, base_ref, out_ref, here_ref, sem):
    blocks = y_ref.shape[0]
    heads = out_ref.shape[1] // HDIM
    wide = heads * HDIM
    feats = w_ref.shape[0] // (2 * blocks)
    chunks = sem.shape[0]
    step = blocks // chunks
    copies = []
    for k in range(chunks):
        rows = pl.ds(k * 2 * step * feats, 2 * step * feats)
        copies.append(pltpu.make_async_copy(w_ref.at[rows], here_ref.at[rows], sem.at[k]))
        copies[-1].start()
    y = y_ref[...].astype(f32)
    fold = spare_row(y[:, :, 0:256], heads, 64).reshape(blocks // 2, 2, ROWS, 256)
    fold = jnp.concatenate([fold[:, 0], fold[:, 1]], axis=-1).reshape(blocks // 2 * ROWS, 512)
    src = iota((512, 128), 0)
    unfold = ((src // 256) * 64 + src % 64 == iota((512, 128), 1)) & (src % 256 < heads * 64)
    odd = jnp.dot(fold.astype(bf16), unfold.astype(bf16), preferred_element_type=f32)
    odd = odd.reshape(blocks // 2, ROWS, 128)
    r = jnp.zeros((ROWS, wide), f32)
    for k in range(chunks):
        copies[k].wait()
        blocks_in = range(k * step, (k + 1) * step)
        left = [y[j] for j in blocks_in] + [odd[j // 2] for j in blocks_in if j % 2 == 0]
        ins = [a for j in blocks_in for a in (2 * j, 2 * j + 1)]
        right = [here_ref[a * feats : a * feats + 256] for a in ins]
        right += [here_ref[a * feats + 256 : (a + 1) * feats] for a in ins]
        r += jnp.dot(
            jnp.concatenate(left, axis=-1).astype(bf16),
            jnp.concatenate(right, axis=0),
            preferred_element_type=f32,
        )
    _, h = rows_of((ROWS, HDIM))
    t = base_ref[...]
    for k in range(heads):
        t += jnp.where(h == k, r[:, k * HDIM : (k + 1) * HDIM], 0.0)
    for k in range(heads):
        both = jnp.concatenate([t[k : k + 1], t[GROUP + k : GROUP + k + 1]], axis=0)
        out_ref[:, k * HDIM : (k + 1) * HDIM] = both.astype(bf16)


def local(
    hidden_rows,
    send_counts,
    row_session,
    row_position,
    resident_lengths,
    kv_weight,
    key_cache,
    value_cache,
    query,
    new_key,
    new_value,
):
    _, insts, cap, feats = hidden_rows.shape
    wide = query.shape[1]
    slots = insts * cap
    blocks = lax.axis_size("head")
    width = feats + 64
    swap = lambda t, axis: lax.all_to_all(t, axis, split_axis=0, concat_axis=0, tiled=True)

    msg, values = pl.pallas_call(
        pack_body,
        out_shape=(
            jax.ShapeDtypeStruct((insts, cap, width), bf16),
            jax.ShapeDtypeStruct((kv_weight.shape[0], wide), bf16),
        ),
        in_specs=vmem(5),
        out_specs=tuple(vmem(2)),
    )(hidden_rows[0], query, send_counts, row_session[0].T, kv_weight)
    values = lax.all_gather(values, "inst", axis=0, tiled=True)
    msg = swap(msg, "inst")

    cache = pl.pallas_call(
        cache_body,
        grid=(1,),
        out_shape=jax.ShapeDtypeStruct((3, ROWS, HDIM), f32),
        in_specs=[pl.BlockSpec(memory_space=pltpu.SMEM)]
        + vmem(3)
        + [pl.BlockSpec((SESS, RES_MAX, wide), lambda i: (0, 0, 0))] * 2,
        out_specs=vmem(1)[0],
    )(resident_lengths, query, new_key, new_value, key_cache, value_cache)

    qw = pl.pallas_call(
        qw_body,
        grid=(1,),
        out_shape=jax.ShapeDtypeStruct((insts, ROWS, 256), bf16),
        in_specs=[pl.BlockSpec((insts, cap, 128), lambda i: (0, 0, width // 128 - 1)), vmem(1)[0]],
        out_specs=vmem(1)[0],
        scratch_shapes=[pltpu.VMEM((128, wide), bf16)],
    )(msg, kv_weight)
    qx = swap(swap(qw, "inst"), "head")

    part, code = pl.pallas_call(
        score_body,
        out_shape=(
            jax.ShapeDtypeStruct((blocks, GROUP, slots), f32),
            jax.ShapeDtypeStruct((ROWS, slots), f32),
        ),
        in_specs=vmem(2),
        out_specs=tuple(vmem(2)),
    )(qx, msg)
    part = swap(part, "head")

    prob, base = pl.pallas_call(
        soft_body,
        out_shape=(
            jax.ShapeDtypeStruct((blocks, GROUP, slots), bf16),
            jax.ShapeDtypeStruct((ROWS, HDIM), f32),
        ),
        in_specs=vmem(3),
        out_specs=tuple(vmem(2)),
    )(part, code, cache)
    prob = swap(prob, "head")

    y = pl.pallas_call(
        mix_body,
        out_shape=jax.ShapeDtypeStruct((blocks, ROWS, 512), bf16),
        in_specs=vmem(3),
        out_specs=vmem(1)[0],
    )(prob, code, msg)
    y = swap(y, "head")

    return pl.pallas_call(
        last_body,
        out_shape=jax.ShapeDtypeStruct((SESS, wide), bf16),
        in_specs=[vmem(1)[0], pl.BlockSpec(memory_space=pl.ANY), vmem(1)[0]],
        out_specs=vmem(1)[0],
        scratch_shapes=[pltpu.VMEM(values.shape, bf16), pltpu.SemaphoreType.DMA((8,))],
        compiler_params=pltpu.CompilerParams(vmem_limit_bytes=56 * 2**20),
    )(y, values, base)


def solution(mesh):
    placed = (
        P("inst", None, None, "head"),
        P("inst", None),
        P("inst", None, None),
        P("inst", None, None),
        P("inst"),
        P("inst", "head"),
        P("inst", None, "head"),
        P("inst", None, "head"),
        P("inst", "head"),
        P("inst", "head"),
        P("inst", "head"),
    )
    return jax.shard_map(
        local, mesh=mesh, in_specs=placed, out_specs=P("inst", "head"), check_vma=False
    )
```

```python
import math

import jax
import jax.numpy as jnp
from jax import lax
from jax.experimental import pallas as pl
from jax.experimental.pallas import tpu as pltpu
from jax.sharding import PartitionSpec as P

HDIM = 128
SESS = 2
RES_MAX = 512
ROWS = 8
GROUP = 4
LOW = -1e30
f32 = jnp.float32
bf16 = jnp.bfloat16
NT = (((1,), (1,)), ((), ()))


def iota(shape, dim):
    return lax.broadcasted_iota(jnp.int32, shape, dim)


def rows_of(shape):
    row = iota(shape, len(shape) - 2) % ROWS
    return row // GROUP, row % GROUP


def spare_row(t, heads, part):
    u, h = rows_of(t.shape)
    own = jnp.where(u == 0, t[..., heads : heads + 1, :], t[..., GROUP + heads : GROUP + heads + 1, :])
    return jnp.where(iota(t.shape, t.ndim - 1) // part == h, own, 0.0)


def near(*arrays):
    return [pltpu.with_memory_space_constraint(a, pltpu.VMEM) for a in arrays]


def vmem(n):
    return [pl.BlockSpec(memory_space=pltpu.VMEM)] * n


def pack_body(x_ref, q_ref, counts_ref, session_ref, w_ref, out_ref, values_ref):
    dests, cap, feats = x_ref.shape
    heads = q_ref.shape[1] // HDIM
    wide = heads * HDIM
    for h in range(heads):
        values_ref[:, h * HDIM : (h + 1) * HDIM] = w_ref[:, (2 * h + 1) * HDIM : (2 * h + 2) * HDIM]
    out_ref[:, :, 0:256] = x_ref[:, :, 0:256]
    out_ref[:, :, 256:512] = x_ref[:, :, 288:544]
    q = q_ref[...].astype(f32)
    row = iota((cap, wide), 0)
    lane = iota((cap, wide), 1)
    spread = jnp.where(row < 8, q[0:1], q[1:2])
    spread = jnp.where((lane % HDIM) // 16 == row % 8, spread, 0.0)
    src = iota((wide, 128), 0)
    dst = iota((wide, 128), 1) - 64
    fold = ((src // HDIM) * 16 + src % 16 == dst).astype(bf16)
    ext = jnp.dot(spread.astype(bf16), fold, preferred_element_type=f32)
    live = iota((cap, dests), 0) < counts_ref[...]
    code = jnp.where(live, 1 + session_ref[...], 0).astype(f32)
    lane = iota((cap, 128), 1)
    none = jnp.zeros((cap, 128 - (feats - 512)), f32)
    for i in range(dests):
        low = x_ref[i, :, 256:384].astype(f32)
        high = jnp.concatenate([x_ref[i, :, 512:feats].astype(f32), none], axis=1)
        t = jnp.where(lane == 64 + 48, code[:, i : i + 1], ext)
        t = jnp.where(lane < 32, low, jnp.where(lane < 64, high, t))
        out_ref[i, :, 512:640] = t.astype(bf16)


def qw_body(msg_ref, w_ref, out_ref, odd_ref):
    sources, cap, width = msg_ref.shape
    heads = w_ref.shape[1] // (2 * HDIM)
    wide = heads * HDIM
    odd_ref[...] = jnp.zeros_like(odd_ref)
    for h in range(heads):
        odd_ref[h * 32 : h * 32 + 32, h * HDIM : (h + 1) * HDIM] = w_ref[256:288, 2 * h * HDIM : (2 * h + 1) * HDIM]
    keys = jnp.concatenate([w_ref[0:256, 2 * h * HDIM : (2 * h + 1) * HDIM] for h in range(heads)], axis=1)

    n = sources * cap
    tail = msg_ref[:, :, width - 128 : width].reshape(n, 128)
    src = iota((128, wide), 0) - 64
    dst = iota((128, wide), 1)
    unfold = ((dst // HDIM) * 16 + dst % 16 == src).astype(bf16)
    z = jnp.dot(tail, unfold, preferred_element_type=f32)
    z = jnp.where((iota((n, wide), 1) % HDIM) // 16 == iota((n, wide), 0) % 8, z, 0.0).astype(bf16)
    m = sources * ROWS
    take = (iota((m, n), 0) // GROUP == iota((m, n), 1) // 8).astype(bf16)
    queries = jnp.dot(take, z, preferred_element_type=f32)
    _, h = rows_of((m, wide))
    queries = jnp.where((iota((m, wide), 1) // HDIM == h) | (h == heads), queries, 0.0).astype(bf16)
    even = lax.dot_general(queries, keys, NT, preferred_element_type=f32)
    odd = lax.dot_general(queries, odd_ref[...], NT, preferred_element_type=f32)
    _, h = rows_of((m, 128))
    first = jnp.where(h == heads, odd, even[:, 0:128])
    out_ref[:, :, 0:128] = first.reshape(sources, ROWS, 128).astype(bf16)
    out_ref[:, :, 128:256] = even[:, 128:256].reshape(sources, ROWS, 128).astype(bf16)


def cache_body(lengths_ref, q_ref, nk_ref, nv_ref, key_ref, value_ref, out_ref):
    heads = q_ref.shape[1] // HDIM
    wide = heads * HDIM
    span = key_ref.shape[1]
    root = 1.0 / math.sqrt(HDIM)
    u, h = rows_of((ROWS, wide))
    mine = iota((ROWS, wide), 1) // HDIM == h
    q = q_ref[...].astype(f32)
    nk = nk_ref[...].astype(f32)
    nv = nv_ref[...].astype(f32)
    scores = jnp.zeros((ROWS, span), f32)
    own = jnp.zeros((ROWS, 1), f32)
    fresh = jnp.zeros((ROWS, wide), f32)
    for s in range(SESS):
        here = mine & (u == s)
        qs = jnp.where(here, q[s : s + 1], 0.0)
        scores += lax.dot_general(qs.astype(bf16), key_ref[s], NT, preferred_element_type=f32)
        own += jnp.sum(qs * nk[s : s + 1], axis=1, keepdims=True)
        fresh += jnp.where(here, nv[s : s + 1], 0.0)
    scores = scores * root
    us, _ = rows_of((ROWS, span))
    length = jnp.where(us == 0, lengths_ref[0], lengths_ref[1])
    seen = iota((ROWS, span), 1) < length
    scores = jnp.where(seen, scores, LOW)
    top = jnp.max(scores, axis=1, keepdims=True)
    weight = jnp.where(seen, jnp.exp(scores - top), 0.0)
    total = jnp.sum(weight, axis=1, keepdims=True)
    high = weight.astype(bf16).astype(f32)
    both = jnp.concatenate([high, weight - high], axis=0)
    us2 = jnp.concatenate([us, us], axis=0)
    acc = jnp.zeros((2 * ROWS, wide), f32)
    for s in range(SESS):
        part = jnp.where(us2 == s, both, 0.0).astype(bf16)
        acc += jnp.dot(part, value_ref[s], preferred_element_type=f32)
    acc = jnp.where(mine, acc[:ROWS] + acc[ROWS:], 0.0)
    out = jnp.zeros((ROWS, HDIM), f32)
    new = jnp.zeros((ROWS, HDIM), f32)
    for k in range(heads):
        out += acc[:, k * HDIM : (k + 1) * HDIM]
        new += fresh[:, k * HDIM : (k + 1) * HDIM]
    out_ref[0] = out
    out_ref[1] = new
    lane = iota((ROWS, HDIM), 1)
    out_ref[2] = jnp.where(lane == 0, top, jnp.where(lane == 1, total, own * root))


def score_body(qx_ref, msg_ref, out_ref, code_ref):
    sources, cap, width = msg_ref.shape
    n = sources * cap
    blocks = qx_ref.shape[0] // 2
    heads = GROUP - 1
    q = qx_ref[...].astype(f32).reshape(blocks, 2, ROWS, 256)
    fold = jnp.concatenate([spare_row(q[:, k, :, 0:128], heads, 32) for k in range(2)], axis=-1)
    src = iota((256, 128), 0)
    unfold = ((src // 128) * 32 + src % 32 == iota((256, 128), 1)) & (src % 128 < heads * 32)
    odd = jnp.dot(
        fold.reshape(blocks * ROWS, 256).astype(bf16), unfold.astype(bf16), preferred_element_type=f32
    )
    even = jnp.concatenate([q[:, 0], q[:, 1]], axis=-1).reshape(blocks * ROWS, 512)
    a = jnp.concatenate([even.astype(bf16), odd.astype(bf16)], axis=-1)
    s = lax.dot_general(a, msg_ref[...].reshape(n, width), NT, preferred_element_type=f32)
    tail = msg_ref[:, :, width - 128 : width].reshape(n, 128)
    one = (iota((ROWS, 128), 1) == 64 + 48).astype(bf16)
    code = lax.dot_general(one, tail, NT, preferred_element_type=f32)
    code_ref[...] = code
    s = s.reshape(blocks, ROWS, n)
    out_ref[...] = jnp.where(code[None, 0:GROUP] == 2.0, s[:, GROUP:ROWS], s[:, 0:GROUP])


def soft_body(parts_ref, code_ref, cache_ref, out_ref, base_ref):
    heads = GROUP - 1
    n = code_ref.shape[1]
    root = 1.0 / math.sqrt(HDIM)
    s = jnp.sum(parts_ref[...], axis=0) * root
    s = jnp.concatenate([s, s], axis=0)
    u, h = rows_of((ROWS, n))
    seen = code_ref[...] == (1 + u).astype(f32)
    s = jnp.where(seen, s, LOW)
    stats = cache_ref[2]
    top_c, total_c, own = stats[:, 0:1], stats[:, 1:2], stats[:, 2:3]
    top = jnp.maximum(jnp.maximum(top_c, own), jnp.max(s, axis=1, keepdims=True))
    weight = jnp.where(seen, jnp.exp(s - top), 0.0)
    scale_c = jnp.exp(top_c - top)
    own_w = jnp.exp(own - top)
    den = jnp.sum(weight, axis=1, keepdims=True) + total_c * scale_c + own_w
    prob = jnp.where(h < heads, weight / den, 0.0)
    prob = prob[0:GROUP] + prob[GROUP:ROWS]
    out_ref[...] = jnp.broadcast_to(prob[None], out_ref.shape).astype(bf16)
    own_p = (own_w / den).astype(bf16).astype(f32)
    base_ref[...] = cache_ref[0] * (scale_c / den) + own_p * cache_ref[1]


def mix_body(prob_ref, code_ref, msg_ref, out_ref):
    sources, cap, width = msg_ref.shape
    n = sources * cap
    blocks = prob_ref.shape[0]
    heads = GROUP - 1
    p = prob_ref[...].astype(f32)
    u, _ = rows_of((ROWS, n))
    p = jnp.where((code_ref[...] == (1 + u).astype(f32))[None], jnp.concatenate([p, p], axis=1), 0.0)
    p = p.reshape(blocks * ROWS, n).astype(bf16)
    y = jnp.dot(p, msg_ref[...].reshape(n, width), preferred_element_type=f32)
    dst = iota((128, 256), 1)
    spread = ((iota((128, 256), 0) == dst % 64) & (dst < heads * 64)).astype(bf16)
    odd = jnp.dot(y[:, 512:640].astype(bf16), spread, preferred_element_type=f32)
    _, h = rows_of((blocks * ROWS, 256))
    odd = jnp.where(dst[0:1] // 64 == h, odd, 0.0).reshape(blocks, ROWS, 256)
    sums = [jnp.sum(odd[:, k : k + GROUP], axis=1, keepdims=True) for k in (0, GROUP)]
    u, h = rows_of((blocks, ROWS, 256))
    y = y.reshape(blocks, ROWS, width)
    first = jnp.where(h == heads, jnp.where(u == 0, sums[0], sums[1]), y[:, :, 0:256])
    out_ref[:, :, 0:256] = first.astype(bf16)
    out_ref[:, :, 256:512] = y[:, :, 256:512].astype(bf16)


def last_body(y_ref, w_ref, base_ref, out_ref, here_ref, sem):
    blocks = y_ref.shape[0]
    heads = out_ref.shape[1] // HDIM
    wide = heads * HDIM
    feats = w_ref.shape[0] // (2 * blocks)
    chunks = sem.shape[0]
    step = blocks // chunks
    copies = []
    for k in range(chunks):
        rows = pl.ds(k * 2 * step * feats, 2 * step * feats)
        copies.append(pltpu.make_async_copy(w_ref.at[rows], here_ref.at[rows], sem.at[k]))
        copies[-1].start()
    y = y_ref[...].astype(f32)
    fold = spare_row(y[:, :, 0:256], heads, 64).reshape(blocks // 2, 2, ROWS, 256)
    fold = jnp.concatenate([fold[:, 0], fold[:, 1]], axis=-1).reshape(blocks // 2 * ROWS, 512)
    src = iota((512, 128), 0)
    unfold = ((src // 256) * 64 + src % 64 == iota((512, 128), 1)) & (src % 256 < heads * 64)
    odd = jnp.dot(fold.astype(bf16), unfold.astype(bf16), preferred_element_type=f32)
    odd = odd.reshape(blocks // 2, ROWS, 128)
    r = jnp.zeros((ROWS, wide), f32)
    for k in range(chunks):
        copies[k].wait()
        blocks_in = range(k * step, (k + 1) * step)
        left = [y[j] for j in blocks_in] + [odd[j // 2] for j in blocks_in if j % 2 == 0]
        ins = [a for j in blocks_in for a in (2 * j, 2 * j + 1)]
        right = [here_ref[a * feats : a * feats + 256] for a in ins]
        right += [here_ref[a * feats + 256 : (a + 1) * feats] for a in ins]
        r += jnp.dot(
            jnp.concatenate(left, axis=-1).astype(bf16),
            jnp.concatenate(right, axis=0),
            preferred_element_type=f32,
        )
    _, h = rows_of((ROWS, HDIM))
    t = base_ref[...]
    for k in range(heads):
        t += jnp.where(h == k, r[:, k * HDIM : (k + 1) * HDIM], 0.0)
    for k in range(heads):
        both = jnp.concatenate([t[k : k + 1], t[GROUP + k : GROUP + k + 1]], axis=0)
        out_ref[:, k * HDIM : (k + 1) * HDIM] = both.astype(bf16)


def local(
    hidden_rows,
    send_counts,
    row_session,
    row_position,
    resident_lengths,
    kv_weight,
    key_cache,
    value_cache,
    query,
    new_key,
    new_value,
):
    _, insts, cap, feats = hidden_rows.shape
    wide = query.shape[1]
    slots = insts * cap
    blocks = lax.axis_size("head")
    width = feats + 64
    swap = lambda t, axis: lax.all_to_all(t, axis, split_axis=0, concat_axis=0, tiled=True)

    msg, values = pl.pallas_call(
        pack_body,
        out_shape=(
            pltpu.VMEM((insts, cap, width), bf16),
            jax.ShapeDtypeStruct((kv_weight.shape[0], wide), bf16),
        ),
        in_specs=vmem(5),
        out_specs=tuple(vmem(2)),
    )(hidden_rows[0], query, send_counts, row_session[0].T, kv_weight)
    values = lax.all_gather(values, "inst", axis=0, tiled=True)
    msg = swap(msg, "inst")

    cache = pl.pallas_call(
        cache_body,
        grid=(1,),
        out_shape=pltpu.VMEM((3, ROWS, HDIM), f32),
        in_specs=[pl.BlockSpec(memory_space=pltpu.SMEM)]
        + vmem(3)
        + [pl.BlockSpec((SESS, RES_MAX, wide), lambda i: (0, 0, 0))] * 2,
        out_specs=vmem(1)[0],
    )(resident_lengths, query, new_key, new_value, key_cache, value_cache)

    qw = pl.pallas_call(
        qw_body,
        out_shape=pltpu.VMEM((insts, ROWS, 256), bf16),
        in_specs=vmem(2),
        out_specs=vmem(1)[0],
        scratch_shapes=[pltpu.VMEM((128, wide), bf16)],
    )(*near(msg), kv_weight)
    qx = swap(swap(qw, "inst"), "head")

    part, code = pl.pallas_call(
        score_body,
        out_shape=(
            pltpu.VMEM((blocks, GROUP, slots), f32),
            pltpu.VMEM((ROWS, slots), f32),
        ),
        in_specs=vmem(2),
        out_specs=tuple(vmem(2)),
    )(*near(qx, msg))
    part = swap(part, "head")

    prob, base = pl.pallas_call(
        soft_body,
        out_shape=(
            pltpu.VMEM((blocks, GROUP, slots), bf16),
            pltpu.VMEM((ROWS, HDIM), f32),
        ),
        in_specs=vmem(3),
        out_specs=tuple(vmem(2)),
    )(*near(part, code, cache))
    prob = swap(prob, "head")

    y = pl.pallas_call(
        mix_body,
        out_shape=pltpu.VMEM((blocks, ROWS, 512), bf16),
        in_specs=vmem(3),
        out_specs=vmem(1)[0],
    )(*near(prob, code, msg))
    y = swap(y, "head")

    return pl.pallas_call(
        last_body,
        out_shape=jax.ShapeDtypeStruct((SESS, wide), bf16),
        in_specs=[vmem(1)[0], pl.BlockSpec(memory_space=pl.ANY), vmem(1)[0]],
        out_specs=vmem(1)[0],
        scratch_shapes=[pltpu.VMEM(values.shape, bf16), pltpu.SemaphoreType.DMA((8,))],
        compiler_params=pltpu.CompilerParams(vmem_limit_bytes=56 * 2**20),
    )(*near(y), values, *near(base))


def solution(mesh):
    placed = (
        P("inst", None, None, "head"),
        P("inst", None),
        P("inst", None, None),
        P("inst", None, None),
        P("inst"),
        P("inst", "head"),
        P("inst", None, "head"),
        P("inst", None, "head"),
        P("inst", "head"),
        P("inst", "head"),
        P("inst", "head"),
    )
    return jax.shard_map(
        local, mesh=mesh, in_specs=placed, out_specs=P("inst", "head"), check_vma=False
    )
```

```python
import math

import jax
import jax.numpy as jnp
from jax import lax
from jax.experimental import pallas as pl
from jax.experimental.pallas import tpu as pltpu
from jax.sharding import PartitionSpec as P

HDIM = 128
SESS = 2
RES_MAX = 512
ROWS = 8
GROUP = 4
LOW = -1e30
f32 = jnp.float32
bf16 = jnp.bfloat16
NT = (((1,), (1,)), ((), ()))


def iota(shape, dim):
    return lax.broadcasted_iota(jnp.int32, shape, dim)


def rows_of(shape):
    row = iota(shape, len(shape) - 2) % ROWS
    return row // GROUP, row % GROUP


def spare_row(t, heads, part):
    u, h = rows_of(t.shape)
    own = jnp.where(u == 0, t[..., heads : heads + 1, :], t[..., GROUP + heads : GROUP + heads + 1, :])
    return jnp.where(iota(t.shape, t.ndim - 1) // part == h, own, 0.0)


def near(*arrays):
    return [pltpu.with_memory_space_constraint(a, pltpu.VMEM) for a in arrays]


def vmem(n):
    return [pl.BlockSpec(memory_space=pltpu.VMEM)] * n


def pack_body(x_ref, q_ref, counts_ref, session_ref, out_ref):
    dests, cap, feats = x_ref.shape
    heads = q_ref.shape[1] // HDIM
    wide = heads * HDIM
    out_ref[:, :, 0:256] = x_ref[:, :, 0:256]
    out_ref[:, :, 256:512] = x_ref[:, :, 288:544]
    q = q_ref[...].astype(f32)
    row = iota((cap, wide), 0)
    lane = iota((cap, wide), 1)
    spread = jnp.where(row < 8, q[0:1], q[1:2])
    spread = jnp.where((lane % HDIM) // 16 == row % 8, spread, 0.0)
    src = iota((wide, 128), 0)
    dst = iota((wide, 128), 1) - 64
    fold = ((src // HDIM) * 16 + src % 16 == dst).astype(bf16)
    ext = jnp.dot(spread.astype(bf16), fold, preferred_element_type=f32)
    live = iota((cap, dests), 0) < counts_ref[...]
    code = jnp.where(live, 1 + session_ref[...], 0).astype(f32)
    lane = iota((cap, 128), 1)
    none = jnp.zeros((cap, 128 - (feats - 512)), f32)
    for i in range(dests):
        low = x_ref[i, :, 256:384].astype(f32)
        high = jnp.concatenate([x_ref[i, :, 512:feats].astype(f32), none], axis=1)
        t = jnp.where(lane == 64 + 48, code[:, i : i + 1], ext)
        t = jnp.where(lane < 32, low, jnp.where(lane < 64, high, t))
        out_ref[i, :, 512:640] = t.astype(bf16)


def qw_body(msg_ref, w_ref, out_ref, odd_ref):
    sources, cap, width = msg_ref.shape
    heads = w_ref.shape[1] // (2 * HDIM)
    wide = heads * HDIM
    odd_ref[...] = jnp.zeros_like(odd_ref)
    for h in range(heads):
        odd_ref[h * 32 : h * 32 + 32, h * HDIM : (h + 1) * HDIM] = w_ref[256:288, 2 * h * HDIM : (2 * h + 1) * HDIM]
    keys = jnp.concatenate([w_ref[0:256, 2 * h * HDIM : (2 * h + 1) * HDIM] for h in range(heads)], axis=1)

    n = sources * cap
    tail = msg_ref[:, :, width - 128 : width].reshape(n, 128)
    src = iota((128, wide), 0) - 64
    dst = iota((128, wide), 1)
    unfold = ((dst // HDIM) * 16 + dst % 16 == src).astype(bf16)
    z = jnp.dot(tail, unfold, preferred_element_type=f32)
    z = jnp.where((iota((n, wide), 1) % HDIM) // 16 == iota((n, wide), 0) % 8, z, 0.0).astype(bf16)
    m = sources * ROWS
    take = (iota((m, n), 0) // GROUP == iota((m, n), 1) // 8).astype(bf16)
    queries = jnp.dot(take, z, preferred_element_type=f32)
    _, h = rows_of((m, wide))
    queries = jnp.where((iota((m, wide), 1) // HDIM == h) | (h == heads), queries, 0.0).astype(bf16)
    even = lax.dot_general(queries, keys, NT, preferred_element_type=f32)
    odd = lax.dot_general(queries, odd_ref[...], NT, preferred_element_type=f32)
    _, h = rows_of((m, 128))
    first = jnp.where(h == heads, odd, even[:, 0:128])
    out_ref[:, :, 0:128] = first.reshape(sources, ROWS, 128).astype(bf16)
    out_ref[:, :, 128:256] = even[:, 128:256].reshape(sources, ROWS, 128).astype(bf16)


def cache_body(lengths_ref, q_ref, nk_ref, nv_ref, key_ref, value_ref, out_ref):
    heads = q_ref.shape[1] // HDIM
    wide = heads * HDIM
    span = key_ref.shape[1]
    root = 1.0 / math.sqrt(HDIM)
    u, h = rows_of((ROWS, wide))
    mine = iota((ROWS, wide), 1) // HDIM == h
    q = q_ref[...].astype(f32)
    nk = nk_ref[...].astype(f32)
    nv = nv_ref[...].astype(f32)
    scores = jnp.zeros((ROWS, span), f32)
    own = jnp.zeros((ROWS, 1), f32)
    fresh = jnp.zeros((ROWS, wide), f32)
    for s in range(SESS):
        here = mine & (u == s)
        qs = jnp.where(here, q[s : s + 1], 0.0)
        scores += lax.dot_general(qs.astype(bf16), key_ref[s], NT, preferred_element_type=f32)
        own += jnp.sum(qs * nk[s : s + 1], axis=1, keepdims=True)
        fresh += jnp.where(here, nv[s : s + 1], 0.0)
    scores = scores * root
    us, _ = rows_of((ROWS, span))
    length = jnp.where(us == 0, lengths_ref[0], lengths_ref[1])
    seen = iota((ROWS, span), 1) < length
    scores = jnp.where(seen, scores, LOW)
    top = jnp.max(scores, axis=1, keepdims=True)
    weight = jnp.where(seen, jnp.exp(scores - top), 0.0)
    total = jnp.sum(weight, axis=1, keepdims=True)
    high = weight.astype(bf16).astype(f32)
    both = jnp.concatenate([high, weight - high], axis=0)
    us2 = jnp.concatenate([us, us], axis=0)
    acc = jnp.zeros((2 * ROWS, wide), f32)
    for s in range(SESS):
        part = jnp.where(us2 == s, both, 0.0).astype(bf16)
        acc += jnp.dot(part, value_ref[s], preferred_element_type=f32)
    acc = jnp.where(mine, acc[:ROWS] + acc[ROWS:], 0.0)
    out = jnp.zeros((ROWS, HDIM), f32)
    new = jnp.zeros((ROWS, HDIM), f32)
    for k in range(heads):
        out += acc[:, k * HDIM : (k + 1) * HDIM]
        new += fresh[:, k * HDIM : (k + 1) * HDIM]
    out_ref[0] = out
    out_ref[1] = new
    lane = iota((ROWS, HDIM), 1)
    out_ref[2] = jnp.where(lane == 0, top, jnp.where(lane == 1, total, own * root))


def score_body(qx_ref, msg_ref, out_ref, code_ref):
    sources, cap, width = msg_ref.shape
    n = sources * cap
    blocks = qx_ref.shape[0] // 2
    heads = GROUP - 1
    q = qx_ref[...].astype(f32).reshape(blocks, 2, ROWS, 256)
    fold = jnp.concatenate([spare_row(q[:, k, :, 0:128], heads, 32) for k in range(2)], axis=-1)
    src = iota((256, 128), 0)
    unfold = ((src // 128) * 32 + src % 32 == iota((256, 128), 1)) & (src % 128 < heads * 32)
    odd = jnp.dot(
        fold.reshape(blocks * ROWS, 256).astype(bf16), unfold.astype(bf16), preferred_element_type=f32
    )
    even = jnp.concatenate([q[:, 0], q[:, 1]], axis=-1).reshape(blocks * ROWS, 512)
    a = jnp.concatenate([even.astype(bf16), odd.astype(bf16)], axis=-1)
    s = lax.dot_general(a, msg_ref[...].reshape(n, width), NT, preferred_element_type=f32)
    tail = msg_ref[:, :, width - 128 : width].reshape(n, 128)
    one = (iota((ROWS, 128), 1) == 64 + 48).astype(bf16)
    code = lax.dot_general(one, tail, NT, preferred_element_type=f32)
    code_ref[...] = code
    s = s.reshape(blocks, ROWS, n)
    out_ref[...] = jnp.where(code[None, 0:GROUP] == 2.0, s[:, GROUP:ROWS], s[:, 0:GROUP])


def soft_body(parts_ref, code_ref, cache_ref, out_ref, base_ref):
    heads = GROUP - 1
    n = code_ref.shape[1]
    root = 1.0 / math.sqrt(HDIM)
    s = jnp.sum(parts_ref[...], axis=0) * root
    s = jnp.concatenate([s, s], axis=0)
    u, h = rows_of((ROWS, n))
    seen = code_ref[...] == (1 + u).astype(f32)
    s = jnp.where(seen, s, LOW)
    stats = cache_ref[2]
    top_c, total_c, own = stats[:, 0:1], stats[:, 1:2], stats[:, 2:3]
    top = jnp.maximum(jnp.maximum(top_c, own), jnp.max(s, axis=1, keepdims=True))
    weight = jnp.where(seen, jnp.exp(s - top), 0.0)
    scale_c = jnp.exp(top_c - top)
    own_w = jnp.exp(own - top)
    den = jnp.sum(weight, axis=1, keepdims=True) + total_c * scale_c + own_w
    prob = jnp.where(h < heads, weight / den, 0.0)
    prob = prob[0:GROUP] + prob[GROUP:ROWS]
    out_ref[...] = jnp.broadcast_to(prob[None], out_ref.shape).astype(bf16)
    own_p = (own_w / den).astype(bf16).astype(f32)
    base_ref[...] = cache_ref[0] * (scale_c / den) + own_p * cache_ref[1]


def mix_body(prob_ref, code_ref, msg_ref, out_ref):
    sources, cap, width = msg_ref.shape
    n = sources * cap
    blocks = prob_ref.shape[0]
    heads = GROUP - 1
    p = prob_ref[...].astype(f32)
    u, _ = rows_of((ROWS, n))
    p = jnp.where((code_ref[...] == (1 + u).astype(f32))[None], jnp.concatenate([p, p], axis=1), 0.0)
    p = p.reshape(blocks * ROWS, n).astype(bf16)
    y = jnp.dot(p, msg_ref[...].reshape(n, width), preferred_element_type=f32)
    dst = iota((128, 256), 1)
    spread = (iota((128, 256), 0) == dst // 128 * 32 + dst % 32) & (dst % 128 < heads * 32)
    odd = jnp.dot(y[:, 512:640].astype(bf16), spread.astype(bf16), preferred_element_type=f32)
    _, h = rows_of((blocks * ROWS, 256))
    odd = jnp.where(dst[0:1] % 128 // 32 == h, odd, 0.0).reshape(blocks, ROWS, 256)
    sums = [jnp.sum(odd[:, k : k + GROUP], axis=1, keepdims=True) for k in (0, GROUP)]
    u, h = rows_of((blocks, ROWS, 256))
    sums = jnp.where(u == 0, sums[0], sums[1])
    spare = h[:, :, 0:128] == heads
    y = y.reshape(blocks, ROWS, width)
    halves = []
    for half in range(2):
        first = jnp.where(spare, sums[:, :, half * 128 : half * 128 + 128], y[:, :, half * 256 : half * 256 + 128])
        halves.append(jnp.concatenate([first, y[:, :, half * 256 + 128 : half * 256 + 256]], axis=-1))
    out_ref[...] = jnp.stack(halves, axis=1).reshape(2 * blocks, ROWS, 256).astype(bf16)


def value_body(y_ref, w_ref, out_ref):
    dests = y_ref.shape[0]
    heads = w_ref.shape[1] // (2 * HDIM)
    m = dests * ROWS
    y = y_ref[...].astype(f32)
    fold = spare_row(y[:, :, 0:128], heads, 32).reshape(m, 128).astype(bf16)
    y = y.reshape(m, 256).astype(bf16)
    columns = [slice((2 * k + 1) * HDIM, (2 * k + 2) * HDIM) for k in range(heads)]
    odd = [w_ref[256:288, c] for c in columns] + [jnp.zeros((128 - heads * 32, HDIM), bf16)]
    out = jnp.dot(fold, jnp.concatenate(odd, axis=0), preferred_element_type=f32)
    even = jnp.concatenate([w_ref[0:256, c] for c in columns], axis=1)
    even = jnp.dot(y, even, preferred_element_type=f32)
    _, h = rows_of((m, HDIM))
    for k in range(heads):
        out += jnp.where(h == k, even[:, k * HDIM : (k + 1) * HDIM], 0.0)
    out_ref[...] = out.reshape(dests, ROWS, HDIM)


def last_body(parts_ref, base_ref, out_ref):
    heads = out_ref.shape[1] // HDIM
    t = jnp.sum(parts_ref[...], axis=0) + base_ref[...]
    for k in range(heads):
        both = jnp.concatenate([t[k : k + 1], t[GROUP + k : GROUP + k + 1]], axis=0)
        out_ref[:, k * HDIM : (k + 1) * HDIM] = both.astype(bf16)


def local(
    hidden_rows,
    send_counts,
    row_session,
    row_position,
    resident_lengths,
    kv_weight,
    key_cache,
    value_cache,
    query,
    new_key,
    new_value,
):
    _, insts, cap, feats = hidden_rows.shape
    wide = query.shape[1]
    slots = insts * cap
    blocks = lax.axis_size("head")
    width = feats + 64
    swap = lambda t, axis: lax.all_to_all(t, axis, split_axis=0, concat_axis=0, tiled=True)

    (weight,) = near(kv_weight)

    msg = pl.pallas_call(
        pack_body,
        out_shape=pltpu.VMEM((insts, cap, width), bf16),
        in_specs=vmem(4),
        out_specs=vmem(1)[0],
    )(hidden_rows[0], query, send_counts, row_session[0].T)
    msg = swap(msg, "inst")

    cache = pl.pallas_call(
        cache_body,
        grid=(1,),
        out_shape=pltpu.VMEM((3, ROWS, HDIM), f32),
        in_specs=[pl.BlockSpec(memory_space=pltpu.SMEM)]
        + vmem(3)
        + [pl.BlockSpec((SESS, RES_MAX, wide), lambda i: (0, 0, 0))] * 2,
        out_specs=vmem(1)[0],
    )(resident_lengths, query, new_key, new_value, key_cache, value_cache)

    qw = pl.pallas_call(
        qw_body,
        out_shape=pltpu.VMEM((insts, ROWS, 256), bf16),
        in_specs=vmem(2),
        out_specs=vmem(1)[0],
        scratch_shapes=[pltpu.VMEM((128, wide), bf16)],
    )(*near(msg), weight)
    qx = swap(swap(qw, "inst"), "head")

    part, code = pl.pallas_call(
        score_body,
        out_shape=(
            pltpu.VMEM((blocks, GROUP, slots), f32),
            pltpu.VMEM((ROWS, slots), f32),
        ),
        in_specs=vmem(2),
        out_specs=tuple(vmem(2)),
    )(*near(qx, msg))
    part = swap(part, "head")

    prob, base = pl.pallas_call(
        soft_body,
        out_shape=(
            pltpu.VMEM((blocks, GROUP, slots), bf16),
            pltpu.VMEM((ROWS, HDIM), f32),
        ),
        in_specs=vmem(3),
        out_specs=tuple(vmem(2)),
    )(*near(part, code, cache))
    prob = swap(prob, "head")

    y = pl.pallas_call(
        mix_body,
        out_shape=pltpu.VMEM((insts, ROWS, 256), bf16),
        in_specs=vmem(3),
        out_specs=vmem(1)[0],
    )(*near(prob, code, msg))
    y = swap(swap(y, "head"), "inst")

    out = pl.pallas_call(
        value_body,
        out_shape=pltpu.VMEM((insts, ROWS, HDIM), f32),
        in_specs=vmem(2),
        out_specs=vmem(1)[0],
    )(*near(y), weight)
    out = swap(out, "inst")

    return pl.pallas_call(
        last_body,
        out_shape=jax.ShapeDtypeStruct((SESS, wide), bf16),
        in_specs=vmem(2),
        out_specs=vmem(1)[0],
    )(*near(out, base))


def solution(mesh):
    placed = (
        P("inst", None, None, "head"),
        P("inst", None),
        P("inst", None, None),
        P("inst", None, None),
        P("inst"),
        P("inst", "head"),
        P("inst", None, "head"),
        P("inst", None, "head"),
        P("inst", "head"),
        P("inst", "head"),
        P("inst", "head"),
    )
    return jax.shard_map(
        local, mesh=mesh, in_specs=placed, out_specs=P("inst", "head"), check_vma=False
    )
```

```python
import math

import jax
import jax.numpy as jnp
from jax import lax
from jax.experimental import pallas as pl
from jax.experimental.pallas import tpu as pltpu
from jax.sharding import PartitionSpec as P

HDIM = 128
SESS = 2
RES_MAX = 512
ROWS = 8
GROUP = 4
LOW = -1e30
f32 = jnp.float32
bf16 = jnp.bfloat16
NT = (((1,), (1,)), ((), ()))


def iota(shape, dim):
    return lax.broadcasted_iota(jnp.int32, shape, dim)


def rows_of(shape):
    row = iota(shape, len(shape) - 2) % ROWS
    return row // GROUP, row % GROUP


def spare_row(t, heads, part):
    u, h = rows_of(t.shape)
    own = jnp.where(u == 0, t[..., heads : heads + 1, :], t[..., GROUP + heads : GROUP + heads + 1, :])
    return jnp.where(iota(t.shape, t.ndim - 1) // part == h, own, 0.0)


def near(*arrays):
    return [pltpu.with_memory_space_constraint(a, pltpu.VMEM) for a in arrays]


def vmem(n):
    return [pl.BlockSpec(memory_space=pltpu.VMEM)] * n


def pack_body(x_ref, q_ref, counts_ref, session_ref, w_ref, out_ref, values_ref):
    dests, cap, feats = x_ref.shape
    heads = q_ref.shape[1] // HDIM
    wide = heads * HDIM
    for h in range(heads):
        values_ref[:, h * HDIM : (h + 1) * HDIM] = w_ref[:, (2 * h + 1) * HDIM : (2 * h + 2) * HDIM]
    out_ref[:, :, 0:256] = x_ref[:, :, 0:256]
    out_ref[:, :, 256:512] = x_ref[:, :, 288:544]
    q = q_ref[...].astype(f32)
    row = iota((cap, wide), 0)
    lane = iota((cap, wide), 1)
    spread = jnp.where(row < 8, q[0:1], q[1:2])
    spread = jnp.where((lane % HDIM) // 16 == row % 8, spread, 0.0)
    src = iota((wide, 128), 0)
    dst = iota((wide, 128), 1) - 64
    fold = ((src // HDIM) * 16 + src % 16 == dst).astype(bf16)
    ext = jnp.dot(spread.astype(bf16), fold, preferred_element_type=f32)
    live = iota((cap, dests), 0) < counts_ref[...]
    code = jnp.where(live, 1 + session_ref[...], 0).astype(f32)
    lane = iota((cap, 128), 1)
    none = jnp.zeros((cap, 128 - (feats - 512)), f32)
    for i in range(dests):
        low = x_ref[i, :, 256:384].astype(f32)
        high = jnp.concatenate([x_ref[i, :, 512:feats].astype(f32), none], axis=1)
        t = jnp.where(lane == 64 + 48, code[:, i : i + 1], ext)
        t = jnp.where(lane < 32, low, jnp.where(lane < 64, high, t))
        out_ref[i, :, 512:640] = t.astype(bf16)


def qw_body(msg_ref, w_ref, out_ref, odd_ref):
    sources, cap, width = msg_ref.shape
    heads = w_ref.shape[1] // (2 * HDIM)
    wide = heads * HDIM
    odd_ref[...] = jnp.zeros_like(odd_ref)
    for h in range(heads):
        odd_ref[h * 32 : h * 32 + 32, h * HDIM : (h + 1) * HDIM] = w_ref[256:288, 2 * h * HDIM : (2 * h + 1) * HDIM]
    keys = jnp.concatenate([w_ref[0:256, 2 * h * HDIM : (2 * h + 1) * HDIM] for h in range(heads)], axis=1)

    n = sources * cap
    tail = msg_ref[:, :, width - 128 : width].reshape(n, 128)
    src = iota((128, wide), 0) - 64
    dst = iota((128, wide), 1)
    unfold = ((dst // HDIM) * 16 + dst % 16 == src).astype(bf16)
    z = jnp.dot(tail, unfold, preferred_element_type=f32)
    z = jnp.where((iota((n, wide), 1) % HDIM) // 16 == iota((n, wide), 0) % 8, z, 0.0).astype(bf16)
    m = sources * ROWS
    take = (iota((m, n), 0) // GROUP == iota((m, n), 1) // 8).astype(bf16)
    queries = jnp.dot(take, z, preferred_element_type=f32)
    _, h = rows_of((m, wide))
    queries = jnp.where((iota((m, wide), 1) // HDIM == h) | (h == heads), queries, 0.0).astype(bf16)
    even = lax.dot_general(queries, keys, NT, preferred_element_type=f32)
    odd = lax.dot_general(queries, odd_ref[...], NT, preferred_element_type=f32)
    _, h = rows_of((m, 128))
    first = jnp.where(h == heads, odd, even[:, 0:128])
    out_ref[:, :, 0:128] = first.reshape(sources, ROWS, 128).astype(bf16)
    out_ref[:, :, 128:256] = even[:, 128:256].reshape(sources, ROWS, 128).astype(bf16)


def cache_body(lengths_ref, q_ref, nk_ref, nv_ref, key_ref, value_ref, out_ref):
    heads = q_ref.shape[1] // HDIM
    wide = heads * HDIM
    span = key_ref.shape[1]
    root = 1.0 / math.sqrt(HDIM)
    u, h = rows_of((ROWS, wide))
    mine = iota((ROWS, wide), 1) // HDIM == h
    q = q_ref[...].astype(f32)
    nk = nk_ref[...].astype(f32)
    nv = nv_ref[...].astype(f32)
    scores = jnp.zeros((ROWS, span), f32)
    own = jnp.zeros((ROWS, 1), f32)
    fresh = jnp.zeros((ROWS, wide), f32)
    for s in range(SESS):
        here = mine & (u == s)
        qs = jnp.where(here, q[s : s + 1], 0.0)
        scores += lax.dot_general(qs.astype(bf16), key_ref[s], NT, preferred_element_type=f32)
        own += jnp.sum(qs * nk[s : s + 1], axis=1, keepdims=True)
        fresh += jnp.where(here, nv[s : s + 1], 0.0)
    scores = scores * root
    us, _ = rows_of((ROWS, span))
    length = jnp.where(us == 0, lengths_ref[0], lengths_ref[1])
    seen = iota((ROWS, span), 1) < length
    scores = jnp.where(seen, scores, LOW)
    top = jnp.max(scores, axis=1, keepdims=True)
    weight = jnp.where(seen, jnp.exp(scores - top), 0.0)
    total = jnp.sum(weight, axis=1, keepdims=True)
    high = weight.astype(bf16).astype(f32)
    both = jnp.concatenate([high, weight - high], axis=0)
    us2 = jnp.concatenate([us, us], axis=0)
    acc = jnp.zeros((2 * ROWS, wide), f32)
    for s in range(SESS):
        part = jnp.where(us2 == s, both, 0.0).astype(bf16)
        acc += jnp.dot(part, value_ref[s], preferred_element_type=f32)
    acc = jnp.where(mine, acc[:ROWS] + acc[ROWS:], 0.0)
    out = jnp.zeros((ROWS, HDIM), f32)
    new = jnp.zeros((ROWS, HDIM), f32)
    for k in range(heads):
        out += acc[:, k * HDIM : (k + 1) * HDIM]
        new += fresh[:, k * HDIM : (k + 1) * HDIM]
    out_ref[0] = out
    out_ref[1] = new
    lane = iota((ROWS, HDIM), 1)
    out_ref[2] = jnp.where(lane == 0, top, jnp.where(lane == 1, total, own * root))


def score_body(qx_ref, msg_ref, out_ref, code_ref):
    sources, cap, width = msg_ref.shape
    n = sources * cap
    blocks = qx_ref.shape[0] // 2
    heads = GROUP - 1
    q = qx_ref[...].astype(f32).reshape(blocks, 2, ROWS, 256)
    fold = jnp.concatenate([spare_row(q[:, k, :, 0:128], heads, 32) for k in range(2)], axis=-1)
    src = iota((256, 128), 0)
    unfold = ((src // 128) * 32 + src % 32 == iota((256, 128), 1)) & (src % 128 < heads * 32)
    odd = jnp.dot(
        fold.reshape(blocks * ROWS, 256).astype(bf16), unfold.astype(bf16), preferred_element_type=f32
    )
    even = jnp.concatenate([q[:, 0], q[:, 1]], axis=-1).reshape(blocks * ROWS, 512)
    a = jnp.concatenate([even.astype(bf16), odd.astype(bf16)], axis=-1)
    s = lax.dot_general(a, msg_ref[...].reshape(n, width), NT, preferred_element_type=f32)
    tail = msg_ref[:, :, width - 128 : width].reshape(n, 128)
    one = (iota((ROWS, 128), 1) == 64 + 48).astype(bf16)
    code = lax.dot_general(one, tail, NT, preferred_element_type=f32)
    code_ref[...] = code
    s = s.reshape(blocks, ROWS, n)
    out_ref[...] = jnp.where(code[None, 0:GROUP] == 2.0, s[:, GROUP:ROWS], s[:, 0:GROUP])


def soft_body(parts_ref, code_ref, cache_ref, out_ref, base_ref):
    heads = GROUP - 1
    n = code_ref.shape[1]
    root = 1.0 / math.sqrt(HDIM)
    s = jnp.sum(parts_ref[...], axis=0) * root
    s = jnp.concatenate([s, s], axis=0)
    u, h = rows_of((ROWS, n))
    seen = code_ref[...] == (1 + u).astype(f32)
    s = jnp.where(seen, s, LOW)
    stats = cache_ref[2]
    top_c, total_c, own = stats[:, 0:1], stats[:, 1:2], stats[:, 2:3]
    top = jnp.maximum(jnp.maximum(top_c, own), jnp.max(s, axis=1, keepdims=True))
    weight = jnp.where(seen, jnp.exp(s - top), 0.0)
    scale_c = jnp.exp(top_c - top)
    own_w = jnp.exp(own - top)
    den = jnp.sum(weight, axis=1, keepdims=True) + total_c * scale_c + own_w
    prob = jnp.where(h < heads, weight / den, 0.0)
    prob = prob[0:GROUP] + prob[GROUP:ROWS]
    out_ref[...] = jnp.broadcast_to(prob[None], out_ref.shape).astype(bf16)
    own_p = (own_w / den).astype(bf16).astype(f32)
    base_ref[...] = cache_ref[0] * (scale_c / den) + own_p * cache_ref[1]


def mix_body(prob_ref, code_ref, msg_ref, out_ref):
    sources, cap, width = msg_ref.shape
    n = sources * cap
    blocks = prob_ref.shape[0]
    heads = GROUP - 1
    p = prob_ref[...].astype(f32)
    u, _ = rows_of((ROWS, n))
    p = jnp.where((code_ref[...] == (1 + u).astype(f32))[None], jnp.concatenate([p, p], axis=1), 0.0)
    p = p.reshape(blocks * ROWS, n).astype(bf16)
    y = jnp.dot(p, msg_ref[...].reshape(n, width), preferred_element_type=f32)
    dst = iota((128, 256), 1)
    spread = ((iota((128, 256), 0) == dst % 64) & (dst < heads * 64)).astype(bf16)
    odd = jnp.dot(y[:, 512:640].astype(bf16), spread, preferred_element_type=f32)
    _, h = rows_of((blocks * ROWS, 256))
    odd = jnp.where(dst[0:1] // 64 == h, odd, 0.0).reshape(blocks, ROWS, 256)
    sums = [jnp.sum(odd[:, k : k + GROUP], axis=1, keepdims=True) for k in (0, GROUP)]
    u, h = rows_of((blocks, ROWS, 256))
    y = y.reshape(blocks, ROWS, width)
    first = jnp.where(h == heads, jnp.where(u == 0, sums[0], sums[1]), y[:, :, 0:256])
    out_ref[:, :, 0:256] = first.astype(bf16)
    out_ref[:, :, 256:512] = y[:, :, 256:512].astype(bf16)


def last_body(y_ref, w_ref, base_ref, out_ref, here_ref, sem):
    blocks = y_ref.shape[0]
    heads = out_ref.shape[1] // HDIM
    wide = heads * HDIM
    feats = w_ref.shape[0] // (2 * blocks)
    chunks = sem.shape[0]
    step = blocks // chunks
    copies = []
    for k in range(chunks):
        rows = pl.ds(k * 2 * step * feats, 2 * step * feats)
        copies.append(pltpu.make_async_copy(w_ref.at[rows], here_ref.at[rows], sem.at[k]))
        copies[-1].start()
    y = y_ref[...].astype(f32)
    fold = spare_row(y[:, :, 0:256], heads, 64).reshape(blocks // 2, 2, ROWS, 256)
    fold = jnp.concatenate([fold[:, 0], fold[:, 1]], axis=-1).reshape(blocks // 2 * ROWS, 512)
    src = iota((512, 128), 0)
    unfold = ((src // 256) * 64 + src % 64 == iota((512, 128), 1)) & (src % 256 < heads * 64)
    odd = jnp.dot(fold.astype(bf16), unfold.astype(bf16), preferred_element_type=f32)
    odd = odd.reshape(blocks // 2, ROWS, 128)
    r = jnp.zeros((ROWS, wide), f32)
    for k in range(chunks):
        copies[k].wait()
        blocks_in = range(k * step, (k + 1) * step)
        left = [y[j] for j in blocks_in] + [odd[j // 2] for j in blocks_in if j % 2 == 0]
        ins = [a for j in blocks_in for a in (2 * j, 2 * j + 1)]
        right = [here_ref[a * feats : a * feats + 256] for a in ins]
        right += [here_ref[a * feats + 256 : (a + 1) * feats] for a in ins]
        r += jnp.dot(
            jnp.concatenate(left, axis=-1).astype(bf16),
            jnp.concatenate(right, axis=0),
            preferred_element_type=f32,
        )
    _, h = rows_of((ROWS, HDIM))
    t = base_ref[...]
    for k in range(heads):
        t += jnp.where(h == k, r[:, k * HDIM : (k + 1) * HDIM], 0.0)
    for k in range(heads):
        both = jnp.concatenate([t[k : k + 1], t[GROUP + k : GROUP + k + 1]], axis=0)
        out_ref[:, k * HDIM : (k + 1) * HDIM] = both.astype(bf16)


def local(
    hidden_rows,
    send_counts,
    row_session,
    row_position,
    resident_lengths,
    kv_weight,
    key_cache,
    value_cache,
    query,
    new_key,
    new_value,
):
    _, insts, cap, feats = hidden_rows.shape
    wide = query.shape[1]
    slots = insts * cap
    blocks = lax.axis_size("head")
    width = feats + 64
    swap = lambda t, axis: lax.all_to_all(t, axis, split_axis=0, concat_axis=0, tiled=True)

    msg, values = pl.pallas_call(
        pack_body,
        out_shape=(
            pltpu.VMEM((insts, cap, width), bf16),
            jax.ShapeDtypeStruct((kv_weight.shape[0], wide), bf16),
        ),
        in_specs=vmem(5),
        out_specs=tuple(vmem(2)),
    )(hidden_rows[0], query, send_counts, row_session[0].T, kv_weight)
    values = lax.all_gather(values, "inst", axis=0, tiled=True)
    msg = swap(msg, "inst")

    cache = pl.pallas_call(
        cache_body,
        grid=(1,),
        out_shape=pltpu.VMEM((3, ROWS, HDIM), f32),
        in_specs=[pl.BlockSpec(memory_space=pltpu.SMEM)]
        + vmem(3)
        + [pl.BlockSpec((SESS, RES_MAX, wide), lambda i: (0, 0, 0))] * 2,
        out_specs=vmem(1)[0],
    )(resident_lengths, query, new_key, new_value, key_cache, value_cache)

    qw = pl.pallas_call(
        qw_body,
        out_shape=pltpu.VMEM((insts, ROWS, 256), bf16),
        in_specs=vmem(2),
        out_specs=vmem(1)[0],
        scratch_shapes=[pltpu.VMEM((128, wide), bf16)],
    )(*near(msg, kv_weight))
    qx = swap(swap(qw, "inst"), "head")

    part, code = pl.pallas_call(
        score_body,
        out_shape=(
            pltpu.VMEM((blocks, GROUP, slots), f32),
            pltpu.VMEM((ROWS, slots), f32),
        ),
        in_specs=vmem(2),
        out_specs=tuple(vmem(2)),
    )(*near(qx, msg))
    part = swap(part, "head")

    prob, base = pl.pallas_call(
        soft_body,
        out_shape=(
            pltpu.VMEM((blocks, GROUP, slots), bf16),
            pltpu.VMEM((ROWS, HDIM), f32),
        ),
        in_specs=vmem(3),
        out_specs=tuple(vmem(2)),
    )(*near(part, code, cache))
    prob = swap(prob, "head")

    y = pl.pallas_call(
        mix_body,
        out_shape=pltpu.VMEM((blocks, ROWS, 512), bf16),
        in_specs=vmem(3),
        out_specs=vmem(1)[0],
    )(*near(prob, code, msg))
    y = swap(y, "head")

    return pl.pallas_call(
        last_body,
        out_shape=jax.ShapeDtypeStruct((SESS, wide), bf16),
        in_specs=[vmem(1)[0], pl.BlockSpec(memory_space=pl.ANY), vmem(1)[0]],
        out_specs=vmem(1)[0],
        scratch_shapes=[pltpu.VMEM(values.shape, bf16), pltpu.SemaphoreType.DMA((8,))],
        compiler_params=pltpu.CompilerParams(vmem_limit_bytes=56 * 2**20),
    )(*near(y), values, *near(base))


def solution(mesh):
    placed = (
        P("inst", None, None, "head"),
        P("inst", None),
        P("inst", None, None),
        P("inst", None, None),
        P("inst"),
        P("inst", "head"),
        P("inst", None, "head"),
        P("inst", None, "head"),
        P("inst", "head"),
        P("inst", "head"),
        P("inst", "head"),
    )
    return jax.shard_map(
        local, mesh=mesh, in_specs=placed, out_specs=P("inst", "head"), check_vma=False
    )
```

```python
import math

import jax
import jax.numpy as jnp
from jax import lax
from jax.experimental import pallas as pl
from jax.experimental.pallas import tpu as pltpu
from jax.sharding import PartitionSpec as P

HDIM = 128
SESS = 2
RES_MAX = 512
ROWS = 8
GROUP = 4
LOW = -1e30
f32 = jnp.float32
bf16 = jnp.bfloat16
NT = (((1,), (1,)), ((), ()))


def iota(shape, dim):
    return lax.broadcasted_iota(jnp.int32, shape, dim)


def rows_of(shape):
    row = iota(shape, len(shape) - 2) % ROWS
    return row // GROUP, row % GROUP


def spare_row(t, heads, part):
    u, h = rows_of(t.shape)
    own = jnp.where(u == 0, t[..., heads : heads + 1, :], t[..., GROUP + heads : GROUP + heads + 1, :])
    return jnp.where(iota(t.shape, t.ndim - 1) // part == h, own, 0.0)


def near(*arrays):
    return [pltpu.with_memory_space_constraint(a, pltpu.VMEM) for a in arrays]


def vmem(n):
    return [pl.BlockSpec(memory_space=pltpu.VMEM)] * n


def pack_body(x_ref, q_ref, counts_ref, session_ref, w_ref, out_ref, values_ref):
    dests, cap, feats = x_ref.shape
    heads = q_ref.shape[1] // HDIM
    wide = heads * HDIM
    for h in range(heads):
        values_ref[:, h * HDIM : (h + 1) * HDIM] = w_ref[:, (2 * h + 1) * HDIM : (2 * h + 2) * HDIM]
    out_ref[:, :, 0:256] = x_ref[:, :, 0:256]
    out_ref[:, :, 256:512] = x_ref[:, :, 288:544]
    q = q_ref[...].astype(f32)
    row = iota((cap, wide), 0)
    lane = iota((cap, wide), 1)
    spread = jnp.where(row < 8, q[0:1], q[1:2])
    spread = jnp.where((lane % HDIM) // 16 == row % 8, spread, 0.0)
    src = iota((wide, 128), 0)
    dst = iota((wide, 128), 1) - 64
    fold = ((src // HDIM) * 16 + src % 16 == dst).astype(bf16)
    ext = jnp.dot(spread.astype(bf16), fold, preferred_element_type=f32)
    live = iota((cap, dests), 0) < counts_ref[...]
    code = jnp.where(live, 1 + session_ref[...], 0).astype(f32)
    lane = iota((cap, 128), 1)
    none = jnp.zeros((cap, 128 - (feats - 512)), f32)
    for i in range(dests):
        low = x_ref[i, :, 256:384].astype(f32)
        high = jnp.concatenate([x_ref[i, :, 512:feats].astype(f32), none], axis=1)
        t = jnp.where(lane == 64 + 48, code[:, i : i + 1], ext)
        t = jnp.where(lane < 32, low, jnp.where(lane < 64, high, t))
        out_ref[i, :, 512:640] = t.astype(bf16)


def qw_body(msg_ref, w_ref, _, out_ref, odd_ref):
    sources, cap, width = msg_ref.shape
    heads = w_ref.shape[1] // (2 * HDIM)
    wide = heads * HDIM
    odd_ref[...] = jnp.zeros_like(odd_ref)
    for h in range(heads):
        odd_ref[h * 32 : h * 32 + 32, h * HDIM : (h + 1) * HDIM] = w_ref[256:288, 2 * h * HDIM : (2 * h + 1) * HDIM]
    keys = jnp.concatenate([w_ref[0:256, 2 * h * HDIM : (2 * h + 1) * HDIM] for h in range(heads)], axis=1)

    n = sources * cap
    tail = msg_ref[:, :, width - 128 : width].reshape(n, 128)
    src = iota((128, wide), 0) - 64
    dst = iota((128, wide), 1)
    unfold = ((dst // HDIM) * 16 + dst % 16 == src).astype(bf16)
    z = jnp.dot(tail, unfold, preferred_element_type=f32)
    z = jnp.where((iota((n, wide), 1) % HDIM) // 16 == iota((n, wide), 0) % 8, z, 0.0).astype(bf16)
    m = sources * ROWS
    take = (iota((m, n), 0) // GROUP == iota((m, n), 1) // 8).astype(bf16)
    queries = jnp.dot(take, z, preferred_element_type=f32)
    _, h = rows_of((m, wide))
    queries = jnp.where((iota((m, wide), 1) // HDIM == h) | (h == heads), queries, 0.0).astype(bf16)
    even = lax.dot_general(queries, keys, NT, preferred_element_type=f32)
    odd = lax.dot_general(queries, odd_ref[...], NT, preferred_element_type=f32)
    _, h = rows_of((m, 128))
    first = jnp.where(h == heads, odd, even[:, 0:128])
    out_ref[:, :, 0:128] = first.reshape(sources, ROWS, 128).astype(bf16)
    out_ref[:, :, 128:256] = even[:, 128:256].reshape(sources, ROWS, 128).astype(bf16)


def cache_body(lengths_ref, q_ref, nk_ref, nv_ref, key_ref, value_ref, out_ref):
    heads = q_ref.shape[1] // HDIM
    wide = heads * HDIM
    span = key_ref.shape[1]
    root = 1.0 / math.sqrt(HDIM)
    u, h = rows_of((ROWS, wide))
    mine = iota((ROWS, wide), 1) // HDIM == h
    q = q_ref[...].astype(f32)
    nk = nk_ref[...].astype(f32)
    nv = nv_ref[...].astype(f32)
    scores = jnp.zeros((ROWS, span), f32)
    own = jnp.zeros((ROWS, 1), f32)
    fresh = jnp.zeros((ROWS, wide), f32)
    for s in range(SESS):
        here = mine & (u == s)
        qs = jnp.where(here, q[s : s + 1], 0.0)
        scores += lax.dot_general(qs.astype(bf16), key_ref[s], NT, preferred_element_type=f32)
        own += jnp.sum(qs * nk[s : s + 1], axis=1, keepdims=True)
        fresh += jnp.where(here, nv[s : s + 1], 0.0)
    scores = scores * root
    us, _ = rows_of((ROWS, span))
    length = jnp.where(us == 0, lengths_ref[0], lengths_ref[1])
    seen = iota((ROWS, span), 1) < length
    scores = jnp.where(seen, scores, LOW)
    top = jnp.max(scores, axis=1, keepdims=True)
    weight = jnp.where(seen, jnp.exp(scores - top), 0.0)
    total = jnp.sum(weight, axis=1, keepdims=True)
    high = weight.astype(bf16).astype(f32)
    both = jnp.concatenate([high, weight - high], axis=0)
    us2 = jnp.concatenate([us, us], axis=0)
    acc = jnp.zeros((2 * ROWS, wide), f32)
    for s in range(SESS):
        part = jnp.where(us2 == s, both, 0.0).astype(bf16)
        acc += jnp.dot(part, value_ref[s], preferred_element_type=f32)
    acc = jnp.where(mine, acc[:ROWS] + acc[ROWS:], 0.0)
    out = jnp.zeros((ROWS, HDIM), f32)
    new = jnp.zeros((ROWS, HDIM), f32)
    for k in range(heads):
        out += acc[:, k * HDIM : (k + 1) * HDIM]
        new += fresh[:, k * HDIM : (k + 1) * HDIM]
    out_ref[0] = out
    out_ref[1] = new
    lane = iota((ROWS, HDIM), 1)
    out_ref[2] = jnp.where(lane == 0, top, jnp.where(lane == 1, total, own * root))


def score_body(qx_ref, msg_ref, out_ref, code_ref):
    sources, cap, width = msg_ref.shape
    n = sources * cap
    blocks = qx_ref.shape[0] // 2
    heads = GROUP - 1
    q = qx_ref[...].astype(f32).reshape(blocks, 2, ROWS, 256)
    fold = jnp.concatenate([spare_row(q[:, k, :, 0:128], heads, 32) for k in range(2)], axis=-1)
    src = iota((256, 128), 0)
    unfold = ((src // 128) * 32 + src % 32 == iota((256, 128), 1)) & (src % 128 < heads * 32)
    odd = jnp.dot(
        fold.reshape(blocks * ROWS, 256).astype(bf16), unfold.astype(bf16), preferred_element_type=f32
    )
    even = jnp.concatenate([q[:, 0], q[:, 1]], axis=-1).reshape(blocks * ROWS, 512)
    a = jnp.concatenate([even.astype(bf16), odd.astype(bf16)], axis=-1)
    s = lax.dot_general(a, msg_ref[...].reshape(n, width), NT, preferred_element_type=f32)
    tail = msg_ref[:, :, width - 128 : width].reshape(n, 128)
    one = (iota((ROWS, 128), 1) == 64 + 48).astype(bf16)
    code = lax.dot_general(one, tail, NT, preferred_element_type=f32)
    code_ref[...] = code
    s = s.reshape(blocks, ROWS, n)
    out_ref[...] = jnp.where(code[None, 0:GROUP] == 2.0, s[:, GROUP:ROWS], s[:, 0:GROUP])


def soft_body(parts_ref, code_ref, cache_ref, out_ref, base_ref):
    heads = GROUP - 1
    n = code_ref.shape[1]
    root = 1.0 / math.sqrt(HDIM)
    s = jnp.sum(parts_ref[...], axis=0) * root
    s = jnp.concatenate([s, s], axis=0)
    u, h = rows_of((ROWS, n))
    seen = code_ref[...] == (1 + u).astype(f32)
    s = jnp.where(seen, s, LOW)
    stats = cache_ref[2]
    top_c, total_c, own = stats[:, 0:1], stats[:, 1:2], stats[:, 2:3]
    top = jnp.maximum(jnp.maximum(top_c, own), jnp.max(s, axis=1, keepdims=True))
    weight = jnp.where(seen, jnp.exp(s - top), 0.0)
    scale_c = jnp.exp(top_c - top)
    own_w = jnp.exp(own - top)
    den = jnp.sum(weight, axis=1, keepdims=True) + total_c * scale_c + own_w
    prob = jnp.where(h < heads, weight / den, 0.0)
    prob = prob[0:GROUP] + prob[GROUP:ROWS]
    out_ref[...] = jnp.broadcast_to(prob[None], out_ref.shape).astype(bf16)
    own_p = (own_w / den).astype(bf16).astype(f32)
    base_ref[...] = cache_ref[0] * (scale_c / den) + own_p * cache_ref[1]


def mix_body(prob_ref, code_ref, msg_ref, out_ref):
    sources, cap, width = msg_ref.shape
    n = sources * cap
    blocks = prob_ref.shape[0]
    heads = GROUP - 1
    p = prob_ref[...].astype(f32)
    u, _ = rows_of((ROWS, n))
    p = jnp.where((code_ref[...] == (1 + u).astype(f32))[None], jnp.concatenate([p, p], axis=1), 0.0)
    p = p.reshape(blocks * ROWS, n).astype(bf16)
    y = jnp.dot(p, msg_ref[...].reshape(n, width), preferred_element_type=f32)
    dst = iota((128, 256), 1)
    spread = ((iota((128, 256), 0) == dst % 64) & (dst < heads * 64)).astype(bf16)
    odd = jnp.dot(y[:, 512:640].astype(bf16), spread, preferred_element_type=f32)
    _, h = rows_of((blocks * ROWS, 256))
    odd = jnp.where(dst[0:1] // 64 == h, odd, 0.0).reshape(blocks, ROWS, 256)
    sums = [jnp.sum(odd[:, k : k + GROUP], axis=1, keepdims=True) for k in (0, GROUP)]
    u, h = rows_of((blocks, ROWS, 256))
    y = y.reshape(blocks, ROWS, width)
    first = jnp.where(h == heads, jnp.where(u == 0, sums[0], sums[1]), y[:, :, 0:256])
    out_ref[:, :, 0:256] = first.astype(bf16)
    out_ref[:, :, 256:512] = y[:, :, 256:512].astype(bf16)


def last_body(y_ref, w_ref, base_ref, out_ref, here_ref, sem):
    blocks = y_ref.shape[0]
    heads = out_ref.shape[1] // HDIM
    wide = heads * HDIM
    feats = w_ref.shape[0] // (2 * blocks)
    chunks = sem.shape[0]
    step = blocks // chunks
    copies = []
    for k in range(chunks):
        rows = pl.ds(k * 2 * step * feats, 2 * step * feats)
        copies.append(pltpu.make_async_copy(w_ref.at[rows], here_ref.at[rows], sem.at[k]))
        copies[-1].start()
    y = y_ref[...].astype(f32)
    fold = spare_row(y[:, :, 0:256], heads, 64).reshape(blocks // 2, 2, ROWS, 256)
    fold = jnp.concatenate([fold[:, 0], fold[:, 1]], axis=-1).reshape(blocks // 2 * ROWS, 512)
    src = iota((512, 128), 0)
    unfold = ((src // 256) * 64 + src % 64 == iota((512, 128), 1)) & (src % 256 < heads * 64)
    odd = jnp.dot(fold.astype(bf16), unfold.astype(bf16), preferred_element_type=f32)
    odd = odd.reshape(blocks // 2, ROWS, 128)
    r = jnp.zeros((ROWS, wide), f32)
    for k in range(chunks):
        copies[k].wait()
        blocks_in = range(k * step, (k + 1) * step)
        left = [y[j] for j in blocks_in] + [odd[j // 2] for j in blocks_in if j % 2 == 0]
        ins = [a for j in blocks_in for a in (2 * j, 2 * j + 1)]
        right = [here_ref[a * feats : a * feats + 256] for a in ins]
        right += [here_ref[a * feats + 256 : (a + 1) * feats] for a in ins]
        r += jnp.dot(
            jnp.concatenate(left, axis=-1).astype(bf16),
            jnp.concatenate(right, axis=0),
            preferred_element_type=f32,
        )
    _, h = rows_of((ROWS, HDIM))
    t = base_ref[...]
    for k in range(heads):
        t += jnp.where(h == k, r[:, k * HDIM : (k + 1) * HDIM], 0.0)
    for k in range(heads):
        both = jnp.concatenate([t[k : k + 1], t[GROUP + k : GROUP + k + 1]], axis=0)
        out_ref[:, k * HDIM : (k + 1) * HDIM] = both.astype(bf16)


def local(
    hidden_rows,
    send_counts,
    row_session,
    row_position,
    resident_lengths,
    kv_weight,
    key_cache,
    value_cache,
    query,
    new_key,
    new_value,
):
    _, insts, cap, feats = hidden_rows.shape
    wide = query.shape[1]
    slots = insts * cap
    blocks = lax.axis_size("head")
    width = feats + 64
    swap = lambda t, axis: lax.all_to_all(t, axis, split_axis=0, concat_axis=0, tiled=True)

    msg, values = pl.pallas_call(
        pack_body,
        out_shape=(
            pltpu.VMEM((insts, cap, width), bf16),
            jax.ShapeDtypeStruct((kv_weight.shape[0], wide), bf16),
        ),
        in_specs=vmem(5),
        out_specs=tuple(vmem(2)),
    )(hidden_rows[0], query, send_counts, row_session[0].T, kv_weight)
    values = lax.all_gather(values, "inst", axis=0, tiled=True)
    msg = swap(msg, "inst")

    cache = pl.pallas_call(
        cache_body,
        grid=(1,),
        out_shape=pltpu.VMEM((3, ROWS, HDIM), f32),
        in_specs=[pl.BlockSpec(memory_space=pltpu.SMEM)]
        + vmem(3)
        + [pl.BlockSpec((SESS, RES_MAX, wide), lambda i: (0, 0, 0))] * 2,
        out_specs=vmem(1)[0],
    )(resident_lengths, query, new_key, new_value, key_cache, value_cache)

    qw = pl.pallas_call(
        qw_body,
        out_shape=pltpu.VMEM((insts, ROWS, 256), bf16),
        in_specs=vmem(3),
        out_specs=vmem(1)[0],
        scratch_shapes=[pltpu.VMEM((128, wide), bf16)],
    )(*near(msg, kv_weight, cache))
    qx = swap(swap(qw, "inst"), "head")

    part, code = pl.pallas_call(
        score_body,
        out_shape=(
            pltpu.VMEM((blocks, GROUP, slots), f32),
            pltpu.VMEM((ROWS, slots), f32),
        ),
        in_specs=vmem(2),
        out_specs=tuple(vmem(2)),
    )(*near(qx, msg))
    part = swap(part, "head")

    prob, base = pl.pallas_call(
        soft_body,
        out_shape=(
            pltpu.VMEM((blocks, GROUP, slots), bf16),
            pltpu.VMEM((ROWS, HDIM), f32),
        ),
        in_specs=vmem(3),
        out_specs=tuple(vmem(2)),
    )(*near(part, code, cache))
    prob = swap(prob, "head")

    y = pl.pallas_call(
        mix_body,
        out_shape=pltpu.VMEM((blocks, ROWS, 512), bf16),
        in_specs=vmem(3),
        out_specs=vmem(1)[0],
    )(*near(prob, code, msg))
    y = swap(y, "head")

    return pl.pallas_call(
        last_body,
        out_shape=jax.ShapeDtypeStruct((SESS, wide), bf16),
        in_specs=[vmem(1)[0], pl.BlockSpec(memory_space=pl.ANY), vmem(1)[0]],
        out_specs=vmem(1)[0],
        scratch_shapes=[pltpu.VMEM(values.shape, bf16), pltpu.SemaphoreType.DMA((8,))],
        compiler_params=pltpu.CompilerParams(vmem_limit_bytes=56 * 2**20),
    )(*near(y), values, *near(base))


def solution(mesh):
    placed = (
        P("inst", None, None, "head"),
        P("inst", None),
        P("inst", None, None),
        P("inst", None, None),
        P("inst"),
        P("inst", "head"),
        P("inst", None, "head"),
        P("inst", None, "head"),
        P("inst", "head"),
        P("inst", "head"),
        P("inst", "head"),
    )
    return jax.shard_map(
        local, mesh=mesh, in_specs=placed, out_specs=P("inst", "head"), check_vma=False
    )
```
